128 devices in a mesh: mp: 4 (over x_hi, core), lat: 32 (over y, z, x_lo).
Axes of the slice: x: 4 (x_hi: 2, x_lo: 2; x = x_hi * 2 + x_lo), y: 4, z: 4, core: 2. Of those that a mesh axis runs over, the one named last changes fastest.
Arguments:
- resid_in: bfloat16 [1024, 2304], P('lat'), may hold values from -6 to 6
- layer_terms: bfloat16 [4, 1024, 2304], P('mp', 'lat'), may hold values from -4 to 4
- dec_bias: float32 [2304], replicated, may hold values from -3 to 3
- enc_weight: bfloat16 [2304, 65536], P(None, ('mp', 'lat')), may hold values from -0.125 to 0.125
- enc_bias: float32 [65536], P(('mp', 'lat')), may hold values from -4.5 to -2
- dec_weight: bfloat16 [65536, 2304], P(('mp', 'lat')), may hold values from -0.25 to 0.25
- first_moment: float32 [2304, 65536], P(None, ('mp', 'lat')), may hold values from -0.6 to 0.6
- second_moment: float32 [2304, 65536], P(None, ('mp', 'lat')), may hold values from 0.002 to 0.3
Outputs:
- enc_weight_new: bfloat16 [2304, 65536], P(None, ('mp', 'lat'))
- first_moment_new: float32 [2304, 65536], P(None, ('mp', 'lat'))
- second_moment_new: float32 [2304, 65536], P(None, ('mp', 'lat'))
- recon_error: bfloat16 [1024, 2304], P(('mp', 'lat'))
The draws below stay inside these ranges and needn't reach their ends.
All inputs are finite; a program needn't handle non-finite values.
Results may differ from the reference program's by a relative error of at most 0.02.
The reference program's roundings to bfloat16 on the way (of `centered`, `codes` and `slopes`) count: a program that leaves them out, or rounds other values in their place, can miss the bound.
Values may be sent and summed in bfloat16 or wider, within the bound.
A program may use at most 128 MiB of HBM per device.

```python
import math
import jax
import jax.numpy as jnp
from jax import lax

D = 2304
LAT_DEV = 512
STEP = 10
LATENTS = 65536
ROWS = 1024
N_MP = 4
N_LAT = 32


def draw_dec_weight(key, part):
    key = jax.random.fold_in(key, 5)
    base_key, scale_key = jax.random.split(key)
    base = jnp.clip(jax.random.normal(base_key, (LATENTS, D), jnp.float32), -4.0, 4.0)
    scales = jnp.exp(jax.random.uniform(scale_key, (LATENTS, 1), jnp.float32, jnp.log(0.3), jnp.log(3.0)))
    return (base * scales / jnp.sqrt(jnp.float32(D))).astype(jnp.bfloat16)


def block_levels(key, extent, cuts, smallest, top_value):
    gain, own = 1.0, jax.random.fold_in(key, 6)
    for dim, blocks in cuts:
        steps = jnp.exp(jax.random.uniform(jax.random.fold_in(own, dim), (blocks,), jnp.float32, smallest / len(cuts), top_value / len(cuts)))
        gain = gain * jnp.repeat(steps, extent[dim] // blocks).reshape([-1 if axis == dim else 1 for axis in range(len(extent))])
    return gain


def bell_draw(rng, shape, scale, reach, shards=(), held_as=jnp.bfloat16):
    level = block_levels(rng, shape, shards, -0.22, 0.18) if shards else 1.0
    values = jax.random.normal(rng, shape, jnp.float32) * scale * level
    return jnp.minimum(jnp.maximum(values, -reach), reach).astype(held_as)


def setup_inputs(seed: int = 0) -> dict:
    arg_keys = jax.random.split(jax.random.key(seed), 9)
    resid_in = bell_draw(arg_keys[0], (ROWS, D), 1.0, 6.0, ((0, 32),))
    layer_terms = bell_draw(arg_keys[1], (N_MP, ROWS, D), 0.5, 4.0, ((0, 4), (1, 32)))
    dec_bias = bell_draw(arg_keys[2], (D,), 0.5, 3.0, (), jnp.float32)
    enc_weight = bell_draw(arg_keys[3], (D, LATENTS), D ** -0.5, 0.125, ((1, 128),))
    enc_bias = jnp.clip(-4.5 + 2.5 * jax.random.uniform(arg_keys[4], (LATENTS,), jnp.float32) ** block_levels(arg_keys[4], (LATENTS,), ((0, 128),), -0.2, 0.2), -4.5, -2.0)
    dec_weight = draw_dec_weight(jax.random.fold_in(arg_keys[8], 71), 0)
    first_moment = bell_draw(arg_keys[6], (D, LATENTS), 0.1, 0.6, ((1, 128),), jnp.float32)
    second_moment = jnp.clip(jnp.exp(math.log(0.3) - 5.0106353 * jax.random.uniform(arg_keys[7], (D, LATENTS), jnp.float32) ** block_levels(arg_keys[7], (D, LATENTS), ((1, 128),), -0.2, 0.2)), 0.002, 0.3)
    return dict(resid_in=resid_in, layer_terms=layer_terms, dec_bias=dec_bias, enc_weight=enc_weight, enc_bias=enc_bias, dec_weight=dec_weight, first_moment=first_moment, second_moment=second_moment)


l1_coeff = 5.0
loss_norm = 32.0
beta_one = 0.9
beta_two = 0.95
learn_rate = 0.001
adam_eps = 1e-08

def reference(resid_in, layer_terms, dec_bias, enc_weight, enc_bias, dec_weight, first_moment, second_moment):
    total = lax.optimization_barrier(jnp.sum(layer_terms.astype(jnp.float32), axis=0))
    centered = (resid_in.astype(jnp.float32) + total - dec_bias).astype(jnp.bfloat16)
    blocks = N_MP * N_LAT
    enc_blocks = enc_weight.reshape(D, blocks, LAT_DEV).transpose(1, 0, 2)
    bias_blocks = enc_bias.reshape(blocks, LAT_DEV)
    dec_blocks = dec_weight.reshape(blocks, LAT_DEV, D)
    first_blocks = first_moment.reshape(D, blocks, LAT_DEV).transpose(1, 0, 2)
    second_blocks = second_moment.reshape(D, blocks, LAT_DEV).transpose(1, 0, 2)

    def encode(weight, bias):
        pre = jnp.dot(centered, weight, preferred_element_type=jnp.float32) + bias
        return jnp.maximum(pre, 0.0).astype(jnp.bfloat16)

    def accumulate(recon, items):
        weight, bias, decoder = items
        codes = encode(weight, bias)
        return (recon + jnp.dot(codes, decoder, preferred_element_type=jnp.float32), None)
    recon, _ = lax.scan(accumulate, jnp.zeros((ROWS, D), jnp.float32), (enc_blocks, bias_blocks, dec_blocks))
    recon_error = (recon - centered.astype(jnp.float32)).astype(jnp.bfloat16)
    corr_one = 1.0 - beta_one ** STEP
    corr_two = 1.0 - beta_two ** STEP

    def update(items):
        weight, bias, decoder, first, second = items
        codes = encode(weight, bias)
        norms = jnp.sqrt(lax.optimization_barrier(jnp.sum(jnp.square(decoder.astype(jnp.float32)), axis=1)))
        back = lax.dot_general(recon_error, decoder, (((1,), (1,)), ((), ())), preferred_element_type=jnp.float32)
        slopes = jnp.where(codes > 0, back * (2.0 / loss_norm) + l1_coeff / loss_norm * norms, 0.0).astype(jnp.bfloat16)
        grad = lax.dot_general(centered, slopes, (((0,), (0,)), ((), ())), preferred_element_type=jnp.float32)
        first_new = beta_one * first + (1.0 - beta_one) * grad
        second_new = beta_two * second + (1.0 - beta_two) * grad * grad
        change = first_new / corr_one / (jnp.sqrt(second_new / corr_two) + adam_eps)
        weight_new = (weight.astype(jnp.float32) - learn_rate * change).astype(jnp.bfloat16)
        return (weight_new, first_new, second_new)
    weight_new, first_new, second_new = lax.map(update, (enc_blocks, bias_blocks, dec_blocks, first_blocks, second_blocks))

    def unblock(array):
        return array.transpose(1, 0, 2).reshape(D, blocks * LAT_DEV)
    return (unblock(weight_new), unblock(first_new), unblock(second_new), recon_error)
```

```python
import jax
import jax.numpy as jnp
from jax import lax
from jax.experimental import pallas as pl
from jax.experimental.pallas import tpu as pltpu
from jax.sharding import PartitionSpec as P

MESH = pl.DeviceIdType.MESH
STEP = 10
l1_coeff = 5.0
loss_norm = 32.0
beta_one = 0.9
beta_two = 0.95
learn_rate = 0.001
adam_eps = 1e-08

D = 2304
HALF = D // 2
GROUP = HALF // 3
PARTS = 3
LAT_DEV = 512
ROWS = 1024
BLOCK = 16
TILE = 256
ORDER = ((2, 1, 0), (0, 2, 1), (1, 0, 2))


def exchange_kernel(
    resid, terms, dec_bias, enc_weight, enc_bias, dec_weight,
    slopes_out, centered_t_out, error_out,
    cen, err, cen_t, weight, dec, dec_t, norms, codes, cross_send, cross_recv, part_sum,
    a_send, a_recv, b_send, b_recv, c_send, c_recv, d_send, d_recv, sum_two, slopes,
    term_in, resid_in, bias_in, enc_bias_in, own_cen,
    send_sems, recv_sems, local_sems,
):
    m = lax.axis_index("mp")
    lat = lax.axis_index("lat")
    core = lax.rem(m, 2)
    yz = lax.div(lat, 2)
    x = lax.div(m, 2) * 2 + lax.rem(lat, 2)
    pos = (x, lax.div(yz, 4), lax.rem(yz, 4))

    def device(at, on_core):
        return (lax.div(at[0], 2) * 2 + on_core, (at[1] * 4 + at[2]) * 2 + lax.rem(at[0], 2))

    def along(axis, k):
        return lax.rem(pos[axis] + k, 4)

    def peer(axis, k):
        at = list(pos)
        at[axis] = along(axis, k)
        return device(at, core)

    other = device(pos, 1 - core)
    g0 = core * PARTS

    count = [0, 0]
    sent = []

    def remote(src, dst, to):
        i = count[0]
        count[0] += 1
        copy = pltpu.make_async_remote_copy(
            src_ref=src, dst_ref=dst, send_sem=send_sems.at[i], recv_sem=recv_sems.at[i],
            device_id=to, device_id_type=MESH,
        )
        copy.start()
        sent.append(copy)
        return copy

    def local(src, dst):
        i = count[1]
        count[1] += 1
        copy = pltpu.make_async_copy(src, dst, local_sems.at[i])
        copy.start()
        return copy

    rows16 = pl.ds(pl.multiple_of(lax.div(m, 2) * BLOCK, BLOCK), BLOCK)
    half = pl.ds(pl.multiple_of(core * HALF, 128), HALF)
    early = [
        local(terms.at[0, rows16, half], term_in.at[0]),
        local(resid.at[rows16, half], resid_in),
        local(dec_bias.at[:, half], bias_in),
        local(enc_bias, enc_bias_in),
    ]
    load_dec = [local(dec_weight.at[:, pl.ds(h * HALF, HALF)], dec.at[h]) for h in range(2)]
    load_weight = local(enc_weight, weight)

    barrier = pltpu.get_barrier_semaphore()
    greet = [other, device((lax.rem(x + 2, 4), pos[1], pos[2]), 1 - core)]
    greet += [peer(axis, k) for axis in range(3) for k in (1, 2, 3)]
    for to in greet:
        pl.semaphore_signal(barrier, inc=1, device_id=to, device_id_type=MESH)
    pl.semaphore_wait(barrier, len(greet))

    moves = []
    for k in (1, 2, 3):
        mt = lax.rem(m + k, 4)
        moves.append(
            remote(
                terms.at[
                    0,
                    pl.ds(pl.multiple_of(lax.div(mt, 2) * BLOCK, BLOCK), BLOCK),
                    pl.ds(pl.multiple_of(lax.rem(mt, 2) * HALF, 128), HALF),
                ],
                term_in.at[k],
                (mt, lat),
            )
        )
    for copy in early:
        copy.wait()
    for copy in moves:
        copy.wait_recv()
    total = term_in[0].astype(jnp.float32)
    for k in (1, 2, 3):
        total = total + term_in[k].astype(jnp.float32)
    own = (resid_in[...].astype(jnp.float32) + total - bias_in[...]).astype(jnp.bfloat16)
    for p in range(PARTS):
        own_cen[p] = own[:, p * GROUP : (p + 1) * GROUP]

    def place(sel):
        return (
            pl.ds(*sel[0]),
            pl.ds(*sel[1]),
            pl.ds(pl.multiple_of(sel[2][0] * BLOCK, BLOCK), sel[2][1] * BLOCK),
        )

    def only(base, axis, start, size):
        sel = list(base)
        sel[axis] = (start, size)
        return sel

    own_sel = [(pos[0], 1), (pos[1], 1), (pos[2], 1)]
    full = [(0, 4), (0, 4), (0, 4)]
    CUT = (1, 0, 0)

    def gather(buf, blocks, fill_one, fill_two, fill_three):
        def at(p, sel):
            return buf.at[(g0 + p,) + place(sel)]

        def share(p, sel, to):
            return remote(at(p, sel), at(p, sel), to)

        for p in range(PARTS):
            buf[(g0 + p,) + place(own_sel)] = blocks[p][None, None]
        one, two, three, four, across = [], [], [], [], []
        for p in range(PARTS):
            one.append([share(p, own_sel, peer(ORDER[p][0], k)) for k in (1, 3, 2)])
        fill_one()
        for p in range(PARTS):
            for copy in one[p]:
                copy.wait_recv()
            sel = only(own_sel, ORDER[p][0], 0, 4)
            two.append([share(p, sel, peer(ORDER[p][1], k)) for k in (1, 3, 2)])
        fill_two()
        for p in range(PARTS):
            for copy in two[p]:
                copy.wait_recv()
            axis = ORDER[p][2]
            sel = only(full, axis, pos[axis], 1)
            three.append([share(p, sel, peer(axis, k)) for k in (1, 3)])
            across.append(share(p, sel, other))
        fill_three()
        for p in range(PARTS):
            axis = ORDER[p][2]
            step = []
            for way, k in ((0, 1), (1, 3)):
                three[p][way].wait_recv()
                sel = only(full, axis, along(axis, 4 - k), 1)
                step.append(share(p, only(sel, CUT[p], way * 2, 2), peer(axis, k)))
                across.append(share(p, sel, other))
            four.append(step)
        for p in range(PARTS):
            axis = ORDER[p][2]
            sel = only(full, axis, along(axis, 2), 1)
            for way in range(2):
                four[p][way].wait_recv()
                across.append(share(p, only(sel, CUT[p], way * 2, 2), other))
        for copy in across:
            copy.wait_recv()

    def nothing():
        pass

    def turn_dec():
        for copy in load_dec:
            copy.wait()

        @pl.loop(0, 2)
        def _(h):
            for q in range(PARTS):
                dec_t[pl.ds(pl.multiple_of(h * HALF + q * GROUP, 128), GROUP), :] = dec[
                    h, :, q * GROUP : (q + 1) * GROUP
                ].T

        norms[...] = jnp.zeros_like(norms)

        @pl.loop(0, 9)
        def _(r):
            rows = dec_t[pl.ds(pl.multiple_of(r * 256, 256), 256), :].astype(jnp.float32)
            norms[...] += jnp.sum(rows * rows, axis=0, keepdims=True)

        norms[...] = jnp.sqrt(norms[...]) * (l1_coeff / loss_norm)

    gather(cen, [own_cen[p] for p in range(PARTS)], nothing, nothing, turn_dec)

    def wide(buf, t):
        return jnp.concatenate([buf[g, t].reshape(TILE, GROUP) for g in range(2 * PARTS)], axis=1)

    load_weight.wait()

    @pl.loop(0, ROWS // TILE)
    def _(t):
        pre = jnp.dot(wide(cen, t), weight[...], preferred_element_type=jnp.float32)
        codes[t] = jnp.maximum(pre + enc_bias_in[...], 0.0).astype(jnp.bfloat16)

    crossing = []
    for t in range(ROWS // TILE):
        made = jnp.dot(codes[t], dec[1 - core], preferred_element_type=jnp.float32)
        for p in range(PARTS):
            cross_send[p, t] = (
                made[:, p * GROUP : (p + 1) * GROUP].astype(jnp.bfloat16).reshape(4, 64, GROUP)
            )
        crossing.append(remote(cross_send.at[:, t], cross_recv.at[:, t], other))

    @pl.loop(0, ROWS // TILE)
    def _(t):
        made = jnp.dot(codes[t], dec[core], preferred_element_type=jnp.float32)
        for p in range(PARTS):
            part_sum[p, t] = made[:, p * GROUP : (p + 1) * GROUP].reshape(4, 64, GROUP)

    for copy in crossing:
        copy.wait_recv()

    def here(p, sel):
        where = (p,) + place(sel)
        value = part_sum[where] + cross_recv[where].astype(jnp.float32)
        return value.reshape(-1, GROUP)

    def turn_centered(first, last):
        @pl.loop(0, ROWS // TILE)
        def _(t):
            for g in range(first, last):
                cen_t[g * GROUP : (g + 1) * GROUP, pl.ds(pl.multiple_of(t * TILE, TILE), TILE)] = (
                    cen[g, t].reshape(TILE, GROUP).T
                )

    step_a = []
    for p in range(PARTS):
        axis = ORDER[p][2]
        far = only(full, axis, along(axis, 2), 1)
        step = []
        for way, k in ((0, 1), (1, 3)):
            a_send[p, way] = here(p, only(far, CUT[p], way * 2, 2)).astype(jnp.bfloat16)
            step.append(remote(a_send.at[p, way], a_recv.at[p, way], peer(axis, k)))
        step_a.append(step)
    turn_centered(0, 2)
    step_b = []
    for p in range(PARTS):
        axis = ORDER[p][2]
        step = []
        for way, k in ((0, 1), (1, 3)):
            step_a[p][way].wait_recv()
            sel = only(full, axis, along(axis, k), 1)
            for part in range(2):
                value = here(p, only(sel, CUT[p], part * 2, 2))
                if part == way:
                    value = value + a_recv[p, way].astype(jnp.float32)
                value = value.astype(jnp.bfloat16)
                b_send[p, way, part] = value
            step.append(remote(b_send.at[p, way], b_recv.at[p, way], peer(axis, k)))
        step_b.append(step)
    turn_centered(2, 4)
    step_c = []
    for p in range(PARTS):
        axis = ORDER[p][2]
        sel = only(full, axis, pos[axis], 1)
        for way in range(2):
            step_b[p][way].wait_recv()
        for part in range(2):
            value = here(p, only(sel, CUT[p], part * 2, 2))
            value = value + b_recv[p, 0, part].astype(jnp.float32) + b_recv[p, 1, part].astype(jnp.float32)
            sum_two[p, part * 2 : part * 2 + 2] = value.reshape(2, 4, BLOCK, GROUP)
        axis = ORDER[p][1]
        step = []
        for j, k in enumerate((1, 3, 2)):
            i = along(axis, k)
            value = sum_two[p, :, i] if p == 1 else sum_two[p, i]
            c_send[p, j] = value.astype(jnp.bfloat16)
            step.append(remote(c_send.at[p, j], c_recv.at[p, j], peer(axis, k)))
        step_c.append(step)
    step_d = []
    kept = []
    for p in range(PARTS):
        axis = ORDER[p][1]
        value = sum_two[p, :, pos[axis]] if p == 1 else sum_two[p, pos[axis]]
        for j in range(3):
            step_c[p][j].wait_recv()
            value = value + c_recv[p, j].astype(jnp.float32)
        sum_two[p, 0] = value
        axis = ORDER[p][0]
        step = []
        for j, k in enumerate((1, 3, 2)):
            d_send[p, j] = sum_two[p, 0, along(axis, k)].astype(jnp.bfloat16)
            step.append(remote(d_send.at[p, j], d_recv.at[p, j], peer(axis, k)))
        step_d.append(step)
    for p in range(PARTS):
        value = sum_two[p, 0, pos[ORDER[p][0]]]
        for j in range(3):
            step_d[p][j].wait_recv()
            value = value + d_recv[p, j].astype(jnp.float32)
        kept.append((value - own_cen[p].astype(jnp.float32)).astype(jnp.bfloat16))

    put = []

    def last_turn():
        turn_centered(4, 6)
        put.append(local(cen_t, centered_t_out))

    gather(err, kept, nothing, nothing, last_turn)

    for t in range(ROWS // TILE):
        back = jnp.dot(wide(err, t), dec_t[...], preferred_element_type=jnp.float32)
        slope = jnp.where(
            codes[t].astype(jnp.float32) > 0.0, back * (2.0 / loss_norm) + norms[...], 0.0
        )
        slopes[t * TILE : (t + 1) * TILE, :] = slope.astype(jnp.bfloat16)
        put.append(
            local(slopes.at[pl.ds(t * TILE, TILE)], slopes_out.at[pl.ds(t * TILE, TILE)])
        )
    row = (m * 32 + lat) * 8
    holder = lax.div(row, 32)
    hx = lax.div(lax.rem(row, 32), BLOCK) * 2 + lax.rem(holder, 2)
    hyz = lax.div(holder, 2)
    hz = pl.ds(pl.multiple_of(lax.rem(hyz, 4) * BLOCK, BLOCK), BLOCK)
    upper = lax.rem(row, BLOCK) > 0
    for g in range(2 * PARTS):
        rows = err[g, hx, lax.div(hyz, 4), hz, :].astype(jnp.float32)
        error_out[:, g * GROUP : (g + 1) * GROUP] = jnp.where(upper, rows[8:], rows[:8])
    for copy in put:
        copy.wait()
    for copy in sent:
        copy.wait_send()


N_REMOTE = 3 + 2 * PARTS * (3 + 3 + 2 + 2 + 5) + 4 + PARTS * (2 + 2 + 3 + 3)
N_LOCAL = 4 + 2 + 1 + 1 + 4


def exchange(resid, terms, dec_bias, enc_weight, enc_bias, dec_weight):
    bf16, f32 = jnp.bfloat16, jnp.float32
    anywhere = pl.BlockSpec(memory_space=pl.ANY)
    return pl.pallas_call(
        exchange_kernel,
        out_shape=(
            jax.ShapeDtypeStruct((ROWS, LAT_DEV), bf16),
            jax.ShapeDtypeStruct((D, ROWS), bf16),
            jax.ShapeDtypeStruct((8, D), f32),
        ),
        in_specs=[anywhere] * 6,
        out_specs=(anywhere, anywhere, pl.BlockSpec(memory_space=pltpu.VMEM)),
        scratch_shapes=[
            pltpu.VMEM((6, 4, 4, 64, GROUP), bf16),
            pltpu.VMEM((6, 4, 4, 64, GROUP), bf16),
            pltpu.VMEM((D, ROWS), bf16),
            pltpu.VMEM((D, LAT_DEV), bf16),
            pltpu.VMEM((2, LAT_DEV, HALF), bf16),
            pltpu.VMEM((D, LAT_DEV), bf16),
            pltpu.VMEM((1, LAT_DEV), f32),
            pltpu.VMEM((4, TILE, LAT_DEV), bf16),
            pltpu.VMEM((PARTS, 4, 4, 64, GROUP), bf16),
            pltpu.VMEM((PARTS, 4, 4, 64, GROUP), bf16),
            pltpu.VMEM((PARTS, 4, 4, 64, GROUP), f32),
            pltpu.VMEM((PARTS, 2, 128, GROUP), bf16),
            pltpu.VMEM((PARTS, 2, 128, GROUP), bf16),
            pltpu.VMEM((PARTS, 2, 2, 128, GROUP), bf16),
            pltpu.VMEM((PARTS, 2, 2, 128, GROUP), bf16),
            pltpu.VMEM((PARTS, 3, 4, BLOCK, GROUP), bf16),
            pltpu.VMEM((PARTS, 3, 4, BLOCK, GROUP), bf16),
            pltpu.VMEM((PARTS, 3, BLOCK, GROUP), bf16),
            pltpu.VMEM((PARTS, 3, BLOCK, GROUP), bf16),
            pltpu.VMEM((PARTS, 4, 4, BLOCK, GROUP), f32),
            pltpu.VMEM((ROWS, LAT_DEV), bf16),
            pltpu.VMEM((4, BLOCK, HALF), bf16),
            pltpu.VMEM((BLOCK, HALF), bf16),
            pltpu.VMEM((1, HALF), f32),
            pltpu.VMEM((1, LAT_DEV), f32),
            pltpu.VMEM((PARTS, BLOCK, GROUP), bf16),
            pltpu.SemaphoreType.DMA((N_REMOTE,)),
            pltpu.SemaphoreType.DMA((N_REMOTE,)),
            pltpu.SemaphoreType.DMA((N_LOCAL,)),
        ],
        compiler_params=pltpu.CompilerParams(
            collective_id=0, has_side_effects=True, vmem_limit_bytes=56 * 1024 * 1024
        ),
    )(resid, terms, dec_bias, enc_weight, enc_bias, dec_weight)


def adam_kernel(cen_t, slopes, weight, first, second, error, weight_new, first_new, second_new, error_new):
    corr_one = 1.0 - beta_one**STEP
    corr_two = 1.0 - beta_two**STEP
    grad = jnp.dot(cen_t[...], slopes[...], preferred_element_type=jnp.float32)
    one = beta_one * first[...] + (1.0 - beta_one) * grad
    two = beta_two * second[...] + (1.0 - beta_two) * grad * grad
    first_new[...] = one
    second_new[...] = two
    change = one / corr_one / (jnp.sqrt(two / corr_two) + adam_eps)
    weight_new[...] = (weight[...].astype(jnp.float32) - learn_rate * change).astype(jnp.bfloat16)

    @pl.when(pl.program_id(0) == 0)
    def _():
        error_new[...] = error[...].astype(jnp.bfloat16)


def adam(cen_t, slopes, weight, first, second, error):
    rows = 256
    tile = pl.BlockSpec((rows, LAT_DEV), lambda i: (i, 0))
    whole_error = pl.BlockSpec((8, D), lambda i: (0, 0))
    return pl.pallas_call(
        adam_kernel,
        grid=(D // rows,),
        out_shape=(
            jax.ShapeDtypeStruct((D, LAT_DEV), jnp.bfloat16),
            jax.ShapeDtypeStruct((D, LAT_DEV), jnp.float32),
            jax.ShapeDtypeStruct((D, LAT_DEV), jnp.float32),
            jax.ShapeDtypeStruct((8, D), jnp.bfloat16),
        ),
        in_specs=[
            pl.BlockSpec((rows, ROWS), lambda i: (i, 0)),
            pl.BlockSpec((ROWS, LAT_DEV), lambda i: (0, 0)),
            tile,
            tile,
            tile,
            whole_error,
        ],
        out_specs=(tile, tile, tile, whole_error),
        compiler_params=pltpu.CompilerParams(vmem_limit_bytes=32 * 1024 * 1024),
    )(cen_t, slopes, weight, first, second, error)


def on_device(
    resid_in, layer_terms, dec_bias, enc_weight, enc_bias, dec_weight, first_moment, second_moment
):
    slopes, cen_t, error = exchange(
        resid_in, layer_terms, dec_bias[None], enc_weight, enc_bias[None], dec_weight
    )
    return adam(cen_t, slopes, enc_weight, first_moment, second_moment, error)


def solution(mesh):
    in_specs = (
        P("lat", None),
        P("mp", "lat", None),
        P(),
        P(None, ("mp", "lat")),
        P(("mp", "lat")),
        P(("mp", "lat"), None),
        P(None, ("mp", "lat")),
        P(None, ("mp", "lat")),
    )
    out_specs = (
        P(None, ("mp", "lat")),
        P(None, ("mp", "lat")),
        P(None, ("mp", "lat")),
        P(("mp", "lat"), None),
    )
    return jax.shard_map(
        on_device, mesh=mesh, in_specs=in_specs, out_specs=out_specs, check_vma=False
    )
```

```python
import jax
import jax.numpy as jnp
from jax import lax
from jax.experimental import pallas as pl
from jax.experimental.pallas import tpu as pltpu
from jax.sharding import PartitionSpec as P

MESH = pl.DeviceIdType.MESH
STEP = 10
l1_coeff = 5.0
loss_norm = 32.0
beta_one = 0.9
beta_two = 0.95
learn_rate = 0.001
adam_eps = 1e-08

D = 2304
HALF = D // 2
GROUP = HALF // 3
PARTS = 3
LAT_DEV = 512
ROWS = 1024
BLOCK = 16
TILE = 256
ORDER = ((2, 1, 0), (0, 2, 1), (1, 0, 2))


def exchange_kernel(
    resid, terms, dec_bias, enc_weight, enc_bias, dec_weight,
    kept_out,
    cen, err, cen_t, weight, dec, dec_t, norms, codes, cross_send, cross_recv, part_sum,
    a_send, a_recv, b_send, b_recv, c_send, c_recv, d_send, d_recv, plane_sum, slopes, half_sum,
    term_in, resid_in, bias_in, enc_bias_in, own_cen, error_rows,
    send_sems, recv_sems, local_sems,
):
    m = lax.axis_index("mp")
    lat = lax.axis_index("lat")
    core = lax.rem(m, 2)
    yz = lax.div(lat, 2)
    x = lax.div(m, 2) * 2 + lax.rem(lat, 2)
    pos = (x, lax.div(yz, 4), lax.rem(yz, 4))

    def device(at, on_core):
        return (lax.div(at[0], 2) * 2 + on_core, (at[1] * 4 + at[2]) * 2 + lax.rem(at[0], 2))

    def along(axis, k):
        return lax.rem(pos[axis] + k, 4)

    def peer(axis, k):
        at = list(pos)
        at[axis] = along(axis, k)
        return device(at, core)

    other = device(pos, 1 - core)
    g0 = core * PARTS

    count = [0, 0]
    sent = []

    def remote(src, dst, to):
        i = count[0]
        count[0] += 1
        copy = pltpu.make_async_remote_copy(
            src_ref=src, dst_ref=dst, send_sem=send_sems.at[i], recv_sem=recv_sems.at[i],
            device_id=to, device_id_type=MESH,
        )
        copy.start()
        sent.append(copy)
        return copy

    def local(src, dst):
        i = count[1]
        count[1] += 1
        copy = pltpu.make_async_copy(src, dst, local_sems.at[i])
        copy.start()
        return copy

    rows16 = pl.ds(pl.multiple_of(lax.div(m, 2) * BLOCK, BLOCK), BLOCK)
    half = pl.ds(pl.multiple_of(core * HALF, 128), HALF)
    early = [
        local(terms.at[0, rows16, half], term_in.at[0]),
        local(resid.at[rows16, half], resid_in),
        local(dec_bias, bias_in),
        local(enc_bias, enc_bias_in),
    ]
    load_dec = [local(dec_weight.at[:, pl.ds(h * HALF, HALF)], dec.at[h]) for h in range(2)]
    load_weight = local(enc_weight, weight)

    barrier = pltpu.get_barrier_semaphore()
    greet = [other, device((lax.rem(x + 2, 4), pos[1], pos[2]), 1 - core)]
    greet += [peer(axis, k) for axis in range(3) for k in (1, 2, 3)]
    for to in greet:
        pl.semaphore_signal(barrier, inc=1, device_id=to, device_id_type=MESH)
    pl.semaphore_wait(barrier, len(greet))

    moves = []
    for k in (1, 2, 3):
        mt = lax.rem(m + k, 4)
        moves.append(
            remote(
                terms.at[
                    0,
                    pl.ds(pl.multiple_of(lax.div(mt, 2) * BLOCK, BLOCK), BLOCK),
                    pl.ds(pl.multiple_of(lax.rem(mt, 2) * HALF, 128), HALF),
                ],
                term_in.at[k],
                (mt, lat),
            )
        )
    for copy in early:
        copy.wait()
    for copy in moves:
        copy.wait_recv()
    total = term_in[0].astype(jnp.float32)
    for k in (1, 2, 3):
        total = total + term_in[k].astype(jnp.float32)
    bias = bias_in[...].reshape(1, D)
    bias = jnp.where(core == 0, bias[:, :HALF], bias[:, HALF:])
    own = (resid_in[...].astype(jnp.float32) + total - bias).astype(jnp.bfloat16)
    for p in range(PARTS):
        own_cen[p] = own[:, p * GROUP : (p + 1) * GROUP]

    def place(sel):
        return (
            pl.ds(*sel[0]),
            pl.ds(*sel[1]),
            pl.ds(pl.multiple_of(sel[2][0] * BLOCK, BLOCK), sel[2][1] * BLOCK),
        )

    def only(base, axis, start, size):
        sel = list(base)
        sel[axis] = (start, size)
        return sel

    own_sel = [(pos[0], 1), (pos[1], 1), (pos[2], 1)]
    full = [(0, 4), (0, 4), (0, 4)]
    ROUTE = ((0, 3), (1, 2))

    def plane(p, k_last, k_second):
        sel = only(full, ORDER[p][2], along(ORDER[p][2], k_last), 1)
        return only(sel, ORDER[p][1], along(ORDER[p][1], k_second), 1)

    def gather(buf, blocks, fill_one, fill_two, fill_three):
        def at(p, sel):
            return buf.at[(g0 + p,) + place(sel)]

        def share(p, sel, to):
            return remote(at(p, sel), at(p, sel), to)

        for p in range(PARTS):
            buf[(g0 + p,) + place(own_sel)] = blocks[p][None, None]
        one, two, across = [], [], []
        three = [[{}, {}] for _ in range(PARTS)]
        four = [[{}, {}] for _ in range(PARTS)]

        def to_neighbours(p, r):
            for way, k in ((0, 1), (1, 3)):
                three[p][way][r] = share(p, plane(p, 0, r), peer(ORDER[p][2], k))

        def onward(p, r):
            for way, k in ((0, 1), (1, 3)):
                three[p][way][r].wait_recv()
                if r in ROUTE[way]:
                    four[p][way][r] = share(p, plane(p, 4 - k, r), peer(ORDER[p][2], k))

        def over(p, k):
            sel = only(full, ORDER[p][2], along(ORDER[p][2], k), 1)
            across.append(share(p, sel, other))

        for p in range(PARTS):
            one.append([share(p, own_sel, peer(ORDER[p][0], k)) for k in (1, 3, 2)])
        fill_one()
        for p in range(PARTS):
            for copy in one[p]:
                copy.wait_recv()
            two.append({k: share(p, plane(p, 0, 0), peer(ORDER[p][1], k)) for k in (1, 3, 2)})
            to_neighbours(p, 0)
        fill_two()
        for k in (1, 3):
            for p in range(PARTS):
                two[p][k].wait_recv()
                to_neighbours(p, 4 - k)
        for p in range(PARTS):
            onward(p, 0)
        for p in range(PARTS):
            two[p][2].wait_recv()
            to_neighbours(p, 2)
            over(p, 0)
        fill_three()
        for r in (3, 1):
            for p in range(PARTS):
                onward(p, r)
        for p in range(PARTS):
            onward(p, 2)
            over(p, 1)
            over(p, 3)
        for way, r in ((0, 0), (0, 3), (1, 1), (1, 2)):
            for p in range(PARTS):
                four[p][way][r].wait_recv()
                across.append(share(p, plane(p, 2, r), other))
        return across

    def nothing():
        pass

    def turn_dec():
        for copy in load_dec:
            copy.wait()

        @pl.loop(0, 2)
        def _(h):
            for q in range(PARTS):
                dec_t[pl.ds(pl.multiple_of(h * HALF + q * GROUP, 128), GROUP), :] = dec[
                    h, :, q * GROUP : (q + 1) * GROUP
                ].T

        norms[...] = jnp.zeros_like(norms)

        @pl.loop(0, 9)
        def _(r):
            rows = dec_t[pl.ds(pl.multiple_of(r * 256, 256), 256), :].astype(jnp.float32)
            norms[...] += jnp.sum(rows * rows, axis=0, keepdims=True)

        norms[...] = jnp.sqrt(norms[...]) * (l1_coeff / loss_norm)

    def wide(buf, t, of_core):
        return jnp.concatenate(
            [buf[of_core * PARTS + p, t].reshape(TILE, GROUP) for p in range(PARTS)], axis=1
        )

    def half_rows(of_core):
        return pl.ds(pl.multiple_of(of_core * HALF, 128), HALF)

    def product(buf, matrix, across, use):
        @pl.loop(0, ROWS // TILE)
        def _(t):
            half_sum[t] = jnp.dot(
                wide(buf, t, core), matrix[half_rows(core), :], preferred_element_type=jnp.float32
            )

        for copy in across:
            copy.wait_recv()
        for t in range(ROWS // TILE):
            use(
                t,
                half_sum[t]
                + jnp.dot(
                    wide(buf, t, 1 - core),
                    matrix[half_rows(1 - core), :],
                    preferred_element_type=jnp.float32,
                ),
            )

    across = gather(cen, [own_cen[p] for p in range(PARTS)], nothing, nothing, turn_dec)
    load_weight.wait()
    keep_weight = local(weight, kept_out.at[pl.ds(D, D), pl.ds(LAT_DEV, LAT_DEV)])
    crossing = []

    def encode(t, pre):
        codes[t] = jnp.maximum(pre + enc_bias_in[...], 0.0).astype(jnp.bfloat16)
        made = jnp.dot(codes[t], dec[1 - core], preferred_element_type=jnp.float32)
        for p in range(PARTS):
            cross_send[p, t] = (
                made[:, p * GROUP : (p + 1) * GROUP].astype(jnp.bfloat16).reshape(4, 64, GROUP)
            )
        crossing.append(remote(cross_send.at[:, t], cross_recv.at[:, t], other))

    product(cen, weight, across, encode)

    @pl.loop(0, ROWS // TILE)
    def _(t):
        made = jnp.dot(codes[t], dec[core], preferred_element_type=jnp.float32)
        for p in range(PARTS):
            part_sum[p, t] = made[:, p * GROUP : (p + 1) * GROUP].reshape(4, 64, GROUP)

    for copy in crossing:
        copy.wait_recv()

    def here(p, sel):
        where = (p,) + place(sel)
        value = part_sum[where] + cross_recv[where].astype(jnp.float32)
        return value.reshape(-1, GROUP)

    def turn_centered(first, last):
        @pl.loop(0, ROWS // TILE)
        def _(t):
            for g in range(first, last):
                cen_t[g * GROUP : (g + 1) * GROUP, pl.ds(pl.multiple_of(t * TILE, TILE), TILE)] = (
                    cen[g, t].reshape(TILE, GROUP).T
                )

    step_a = [[{}, {}] for _ in range(PARTS)]
    step_b = [[{}, {}] for _ in range(PARTS)]
    for way, k in ((0, 1), (1, 3)):
        for r in ROUTE[way]:
            for p in range(PARTS):
                a_send[p, r] = here(p, plane(p, 2, r)).astype(jnp.bfloat16)
                step_a[p][way][r] = remote(a_send.at[p, r], a_recv.at[p, r], peer(ORDER[p][2], k))

    def to_owner(p, way, k, r):
        value = here(p, plane(p, k, r))
        if r in ROUTE[way]:
            step_a[p][way][r].wait_recv()
            value = value + a_recv[p, r].astype(jnp.float32)
        b_send[p, way, r] = value.astype(jnp.bfloat16)
        step_b[p][way][r] = remote(b_send.at[p, way, r], b_recv.at[p, way, r], peer(ORDER[p][2], k))

    for way, k in ((0, 1), (1, 3)):
        for r in ROUTE[1 - way]:
            for p in range(PARTS):
                to_owner(p, way, k, r)
    turn_centered(0, 2)
    for way, k in ((0, 1), (1, 3)):
        for r in ROUTE[way]:
            for p in range(PARTS):
                to_owner(p, way, k, r)
    turn_centered(2, 4)
    step_c = [{} for _ in range(PARTS)]
    for r in (3, 1, 2, 0):
        for p in range(PARTS):
            value = here(p, plane(p, 0, r))
            for way in range(2):
                step_b[p][way][r].wait_recv()
                value = value + b_recv[p, way, r].astype(jnp.float32)
            if r:
                c_send[p, r - 1] = value.astype(jnp.bfloat16)
                step_c[p][r] = remote(c_send.at[p, r - 1], c_recv.at[p, r - 1], peer(ORDER[p][1], r))
            else:
                plane_sum[p] = value.reshape(4, BLOCK, GROUP)
    step_d = []
    kept = []
    for p in range(PARTS):
        value = plane_sum[p]
        for r in (3, 1, 2):
            step_c[p][r].wait_recv()
            value = value + c_recv[p, r - 1].astype(jnp.float32).reshape(4, BLOCK, GROUP)
        plane_sum[p] = value
        axis = ORDER[p][0]
        step = []
        for j, k in enumerate((1, 3, 2)):
            d_send[p, j] = plane_sum[p, along(axis, k)].astype(jnp.bfloat16)
            step.append(remote(d_send.at[p, j], d_recv.at[p, j], peer(axis, k)))
        step_d.append(step)
    for p in range(PARTS):
        value = plane_sum[p, pos[ORDER[p][0]]]
        for j in range(3):
            step_d[p][j].wait_recv()
            value = value + d_recv[p, j].astype(jnp.float32)
        kept.append((value - own_cen[p].astype(jnp.float32)).astype(jnp.bfloat16))

    put = [keep_weight]

    def last_turn():
        turn_centered(4, 6)
        put.append(local(cen_t, kept_out.at[pl.ds(0, D)]))

    across = gather(err, kept, nothing, nothing, last_turn)

    def slope_of(t, back):
        slope = jnp.where(
            codes[t].astype(jnp.float32) > 0.0, back * (2.0 / loss_norm) + norms[...], 0.0
        )
        slopes[t * TILE : (t + 1) * TILE, :] = slope.astype(jnp.bfloat16)
        put.append(
            local(
                slopes.at[pl.ds(t * TILE, TILE)],
                kept_out.at[pl.ds(D + t * TILE, TILE), pl.ds(0, LAT_DEV)],
            )
        )

    product(err, dec_t, across, slope_of)
    row = (m * 32 + lat) * 8
    holder = lax.div(row, 32)
    hx = lax.div(lax.rem(row, 32), BLOCK) * 2 + lax.rem(holder, 2)
    hyz = lax.div(holder, 2)
    hz = pl.ds(pl.multiple_of(lax.rem(hyz, 4) * BLOCK, BLOCK), BLOCK)
    upper = lax.rem(row, BLOCK) > 0
    for g in range(2 * PARTS):
        rows = err[g, hx, lax.div(hyz, 4), hz, :].astype(jnp.float32)
        rows = jnp.where(upper, rows[8:], rows[:8])
        error_rows[:, g * GROUP : (g + 1) * GROUP] = jnp.concatenate([rows, rows]).astype(jnp.bfloat16)
    for i in range(3):
        put.append(
            local(
                error_rows.at[:, pl.ds(i * 768, 768)],
                kept_out.at[pl.ds(2 * D + i * BLOCK, BLOCK), pl.ds(0, 768)],
            )
        )
    for copy in put:
        copy.wait()
    for copy in sent:
        copy.wait_send()


N_REMOTE = 3 + 2 * PARTS * (3 + 3 + 8 + 4 + 7) + 4 + PARTS * (4 + 8 + 3 + 3)
N_LOCAL = 4 + 2 + 1 + 1 + 1 + 4 + 3
KEPT = 8192


def exchange(resid, terms, dec_bias, enc_weight, enc_bias, dec_weight):
    bf16, f32 = jnp.bfloat16, jnp.float32
    anywhere = pl.BlockSpec(memory_space=pl.ANY)
    hbm = pl.BlockSpec(memory_space=pltpu.HBM)
    return pl.pallas_call(
        exchange_kernel,
        out_shape=jax.ShapeDtypeStruct((KEPT, ROWS), bf16),
        in_specs=[hbm] * 6,
        out_specs=anywhere,
        scratch_shapes=[
            pltpu.VMEM((6, 4, 4, 64, GROUP), bf16),
            pltpu.VMEM((6, 4, 4, 64, GROUP), bf16),
            pltpu.VMEM((D, ROWS), bf16),
            pltpu.VMEM((D, LAT_DEV), bf16),
            pltpu.VMEM((2, LAT_DEV, HALF), bf16),
            pltpu.VMEM((D, LAT_DEV), bf16),
            pltpu.VMEM((1, LAT_DEV), f32),
            pltpu.VMEM((4, TILE, LAT_DEV), bf16),
            pltpu.VMEM((PARTS, 4, 4, 64, GROUP), bf16),
            pltpu.VMEM((PARTS, 4, 4, 64, GROUP), bf16),
            pltpu.VMEM((PARTS, 4, 4, 64, GROUP), f32),
            pltpu.VMEM((PARTS, 4, 64, GROUP), bf16),
            pltpu.VMEM((PARTS, 4, 64, GROUP), bf16),
            pltpu.VMEM((PARTS, 2, 4, 64, GROUP), bf16),
            pltpu.VMEM((PARTS, 2, 4, 64, GROUP), bf16),
            pltpu.VMEM((PARTS, 3, 64, GROUP), bf16),
            pltpu.VMEM((PARTS, 3, 64, GROUP), bf16),
            pltpu.VMEM((PARTS, 3, BLOCK, GROUP), bf16),
            pltpu.VMEM((PARTS, 3, BLOCK, GROUP), bf16),
            pltpu.VMEM((PARTS, 4, BLOCK, GROUP), f32),
            pltpu.VMEM((ROWS, LAT_DEV), bf16),
            pltpu.VMEM((4, TILE, LAT_DEV), f32),
            pltpu.VMEM((4, BLOCK, HALF), bf16),
            pltpu.VMEM((BLOCK, HALF), bf16),
            pltpu.VMEM((D,), f32),
            pltpu.VMEM((1, LAT_DEV), f32),
            pltpu.VMEM((PARTS, BLOCK, GROUP), bf16),
            pltpu.VMEM((BLOCK, D), bf16),
            pltpu.SemaphoreType.DMA((N_REMOTE,)),
            pltpu.SemaphoreType.DMA((N_REMOTE,)),
            pltpu.SemaphoreType.DMA((N_LOCAL,)),
        ],
        cost_estimate=pl.CostEstimate(flops=90_000_000_000, bytes_accessed=10_000_000, transcendentals=0),
        compiler_params=pltpu.CompilerParams(
            collective_id=0, has_side_effects=True, vmem_limit_bytes=54 * 1024 * 1024
        ),
    )(resid, terms, dec_bias, enc_weight, enc_bias, dec_weight)


TILES = D // TILE


def adam_kernel(
    kept, first, second,
    weight_new, first_new, second_new, error_new,
    cen_in, slopes_in, weight_in, one_in, two_in, error_in, weight_out, one_out, two_out,
    in_sems, out_sems, lone_sems,
):
    def tile(t):
        return pl.ds(t * TILE, TILE)

    load_slopes = pltpu.make_async_copy(
        kept.at[pl.ds(D, ROWS), pl.ds(0, LAT_DEV)], slopes_in, lone_sems.at[0]
    )
    load_slopes.start()
    loads = []
    for t in range(TILES):
        pairs = (
            (kept.at[tile(t)], cen_in),
            (kept.at[pl.ds(D + t * TILE, TILE), pl.ds(LAT_DEV, LAT_DEV)], weight_in),
            (first.at[tile(t)], one_in),
            (second.at[tile(t)], two_in),
        )
        step = [
            pltpu.make_async_copy(src, dst.at[tile(t)], in_sems.at[i, t])
            for i, (src, dst) in enumerate(pairs)
        ]
        for copy in step:
            copy.start()
        loads.append(step)
    load_error = [
        pltpu.make_async_copy(
            kept.at[pl.ds(2 * D + i * BLOCK, BLOCK), pl.ds(0, 768)],
            error_in.at[:, pl.ds(i * 768, 768)],
            lone_sems.at[1 + i],
        )
        for i in range(3)
    ]
    for copy in load_error:
        copy.start()
    load_slopes.wait()
    corr_one = 1.0 - beta_one**STEP
    corr_two = 1.0 - beta_two**STEP
    stores = []
    for t in range(TILES):
        for copy in loads[t]:
            copy.wait()
        rows = tile(t)
        grad = jnp.dot(cen_in[rows], slopes_in[...], preferred_element_type=jnp.float32)
        one = beta_one * one_in[rows] + (1.0 - beta_one) * grad
        two = beta_two * two_in[rows] + (1.0 - beta_two) * grad * grad
        one_out[rows] = one
        two_out[rows] = two
        scaled = two * (1.0 / corr_two)
        change = one * (learn_rate / corr_one) / (scaled * lax.rsqrt(scaled) + adam_eps)
        weight_out[rows] = (weight_in[rows].astype(jnp.float32) - change).astype(jnp.bfloat16)
        pairs = ((one_out, first_new), (two_out, second_new), (weight_out, weight_new))
        for i, (src, dst) in enumerate(pairs):
            copy = pltpu.make_async_copy(src.at[rows], dst.at[rows], out_sems.at[i, t])
            copy.start()
            stores.append(copy)
    for copy in load_error:
        copy.wait()
    error_new[...] = error_in[:8, :]
    for copy in stores:
        copy.wait()


def adam(kept, first, second):
    bf16, f32 = jnp.bfloat16, jnp.float32
    anywhere = pl.BlockSpec(memory_space=pl.ANY)
    hbm = pl.BlockSpec(memory_space=pltpu.HBM)
    return pl.pallas_call(
        adam_kernel,
        out_shape=(
            jax.ShapeDtypeStruct((D, LAT_DEV), bf16),
            jax.ShapeDtypeStruct((D, LAT_DEV), f32),
            jax.ShapeDtypeStruct((D, LAT_DEV), f32),
            jax.ShapeDtypeStruct((8, D), bf16),
        ),
        in_specs=[anywhere] * 3,
        out_specs=(hbm, hbm, hbm, pl.BlockSpec(memory_space=pltpu.VMEM)),
        scratch_shapes=[
            pltpu.VMEM((D, ROWS), bf16),
            pltpu.VMEM((ROWS, LAT_DEV), bf16),
            pltpu.VMEM((D, LAT_DEV), bf16),
            pltpu.VMEM((D, LAT_DEV), f32),
            pltpu.VMEM((D, LAT_DEV), f32),
            pltpu.VMEM((BLOCK, D), bf16),
            pltpu.VMEM((D, LAT_DEV), bf16),
            pltpu.VMEM((D, LAT_DEV), f32),
            pltpu.VMEM((D, LAT_DEV), f32),
            pltpu.SemaphoreType.DMA((4, TILES)),
            pltpu.SemaphoreType.DMA((3, TILES)),
            pltpu.SemaphoreType.DMA((4,)),
        ],
        cost_estimate=pl.CostEstimate(
            flops=2 * ROWS * D * LAT_DEV, bytes_accessed=29_000_000, transcendentals=0
        ),
        compiler_params=pltpu.CompilerParams(vmem_limit_bytes=44 * 1024 * 1024),
    )(kept, first, second)


def on_device(
    resid_in, layer_terms, dec_bias, enc_weight, enc_bias, dec_weight, first_moment, second_moment
):
    kept = exchange(
        resid_in, layer_terms, dec_bias, enc_weight, enc_bias[None], dec_weight
    )
    return adam(kept, first_moment, second_moment)


def solution(mesh):
    in_specs = (
        P("lat", None),
        P("mp", "lat", None),
        P(),
        P(None, ("mp", "lat")),
        P(("mp", "lat")),
        P(("mp", "lat"), None),
        P(None, ("mp", "lat")),
        P(None, ("mp", "lat")),
    )
    out_specs = (
        P(None, ("mp", "lat")),
        P(None, ("mp", "lat")),
        P(None, ("mp", "lat")),
        P(("mp", "lat"), None),
    )
    return jax.shard_map(
        on_device, mesh=mesh, in_specs=in_specs, out_specs=out_specs, check_vma=False
    )
```

```python
import jax
import jax.numpy as jnp
from jax import lax
from jax.experimental import pallas as pl
from jax.experimental.pallas import tpu as pltpu
from jax.sharding import PartitionSpec as P

MESH = pl.DeviceIdType.MESH
STEP = 10
l1_coeff = 5.0
loss_norm = 32.0
beta_one = 0.9
beta_two = 0.95
learn_rate = 0.001
adam_eps = 1e-08

D = 2304
HALF = D // 2
GROUP = HALF // 3
PARTS = 3
LAT_DEV = 512
ROWS = 1024
BLOCK = 16
TILE = 256
ORDER = ((2, 1, 0), (0, 2, 1), (1, 0, 2))


def exchange_kernel(
    resid, terms, dec_bias, enc_weight, enc_bias, dec_weight,
    kept_out,
    cen, err, cen_t, weight, dec, dec_t, norms, codes, cross_send, cross_recv, part_sum,
    a_send, a_recv, b_send, b_recv, c_send, c_recv, plane_sum, slopes, half_sum,
    term_in, resid_in, bias_in, enc_bias_in, own_cen, error_rows,
    send_sems, recv_sems, local_sems,
):
    m = lax.axis_index("mp")
    lat = lax.axis_index("lat")
    core = lax.rem(m, 2)
    yz = lax.div(lat, 2)
    x = lax.div(m, 2) * 2 + lax.rem(lat, 2)
    pos = (x, lax.div(yz, 4), lax.rem(yz, 4))

    def device(at, on_core):
        return (lax.div(at[0], 2) * 2 + on_core, (at[1] * 4 + at[2]) * 2 + lax.rem(at[0], 2))

    def along(axis, k):
        return lax.rem(pos[axis] + k, 4)

    def peer(axis, k):
        at = list(pos)
        at[axis] = along(axis, k)
        return device(at, core)

    other = device(pos, 1 - core)
    g0 = core * PARTS

    count = [0, 0]
    sent = []

    def remote(src, dst, to):
        i = count[0]
        count[0] += 1
        copy = pltpu.make_async_remote_copy(
            src_ref=src, dst_ref=dst, send_sem=send_sems.at[i], recv_sem=recv_sems.at[i],
            device_id=to, device_id_type=MESH,
        )
        copy.start()
        sent.append(copy)
        return copy

    def local(src, dst):
        i = count[1]
        count[1] += 1
        copy = pltpu.make_async_copy(src, dst, local_sems.at[i])
        copy.start()
        return copy

    rows16 = pl.ds(pl.multiple_of(lax.div(m, 2) * BLOCK, BLOCK), BLOCK)
    half = pl.ds(pl.multiple_of(core * HALF, 128), HALF)
    early = [
        local(terms.at[0, rows16, half], term_in.at[0]),
        local(resid.at[rows16, half], resid_in),
        local(dec_bias, bias_in),
        local(enc_bias, enc_bias_in),
    ]
    load_dec = [local(dec_weight.at[:, pl.ds(h * HALF, HALF)], dec.at[h]) for h in range(2)]
    load_weight = local(enc_weight, weight)

    barrier = pltpu.get_barrier_semaphore()
    greet = [other, device((lax.rem(x + 2, 4), pos[1], pos[2]), 1 - core)]
    greet += [peer(axis, k) for axis in range(3) for k in (1, 2, 3)]
    for to in greet:
        pl.semaphore_signal(barrier, inc=1, device_id=to, device_id_type=MESH)
    pl.semaphore_wait(barrier, len(greet))

    moves = []
    for k in (1, 2, 3):
        mt = lax.rem(m + k, 4)
        moves.append(
            remote(
                terms.at[
                    0,
                    pl.ds(pl.multiple_of(lax.div(mt, 2) * BLOCK, BLOCK), BLOCK),
                    pl.ds(pl.multiple_of(lax.rem(mt, 2) * HALF, 128), HALF),
                ],
                term_in.at[k],
                (mt, lat),
            )
        )
    for copy in early:
        copy.wait()
    for copy in moves:
        copy.wait_recv()
    total = term_in[0].astype(jnp.float32)
    for k in (1, 2, 3):
        total = total + term_in[k].astype(jnp.float32)
    bias = bias_in[...].reshape(1, D)
    bias = jnp.where(core == 0, bias[:, :HALF], bias[:, HALF:])
    own = (resid_in[...].astype(jnp.float32) + total - bias).astype(jnp.bfloat16)
    for p in range(PARTS):
        own_cen[p] = own[:, p * GROUP : (p + 1) * GROUP]

    def place(sel):
        return (
            pl.ds(*sel[0]),
            pl.ds(*sel[1]),
            pl.ds(pl.multiple_of(sel[2][0] * BLOCK, BLOCK), sel[2][1] * BLOCK),
        )

    def only(base, axis, start, size):
        sel = list(base)
        sel[axis] = (start, size)
        return sel

    own_sel = [(pos[0], 1), (pos[1], 1), (pos[2], 1)]
    full = [(0, 4), (0, 4), (0, 4)]
    ROUTE = ((0,), (3,))
    STRAIGHT = (1, 2)
    STEPS = (0, 1, 3, 2)

    def plane(p, k_last, k_second):
        sel = only(full, ORDER[p][2], along(ORDER[p][2], k_last), 1)
        return only(sel, ORDER[p][1], along(ORDER[p][1], k_second), 1)

    def across_plane(p, q, r):
        at = list(pos)
        at[ORDER[p][0]] = along(ORDER[p][0], q)
        at[ORDER[p][1]] = along(ORDER[p][1], r)
        return device(at, core)

    def gather(buf, blocks, fill_one, fill_two):
        def at(p, sel):
            return buf.at[(g0 + p,) + place(sel)]

        def share(p, sel, to):
            return remote(at(p, sel), at(p, sel), to)

        for p in range(PARTS):
            buf[(g0 + p,) + place(own_sel)] = blocks[p][None, None]
        across = []
        first = []
        second = []
        three = [[{}, {}, {}] for _ in range(PARTS)]
        four = [[{}, {}] for _ in range(PARTS)]

        def to_neighbours(p, r):
            for way, k in ((0, 1), (1, 3)):
                three[p][way][r] = share(p, plane(p, 0, r), peer(ORDER[p][2], k))
            if r in STRAIGHT:
                three[p][2][r] = share(p, plane(p, 0, r), peer(ORDER[p][2], 2))

        def onward(p, way, r):
            k = (1, 3)[way]
            three[p][way][r].wait_recv()
            four[p][way][r] = share(p, plane(p, 4 - k, r), peer(ORDER[p][2], k))

        def over(p, k):
            sel = only(full, ORDER[p][2], along(ORDER[p][2], k), 1)
            across.append(share(p, sel, other))

        for p in range(PARTS):
            first.append([share(p, own_sel, peer(ORDER[p][0], k)) for k in (1, 3, 2)])
        fill_one()
        for p in range(PARTS):
            for copy in first[p]:
                copy.wait_recv()
            second.append({k: share(p, plane(p, 0, 0), peer(ORDER[p][1], k)) for k in (1, 3, 2)})
            to_neighbours(p, 0)
        for k in (1, 3):
            for p in range(PARTS):
                second[p][k].wait_recv()
                to_neighbours(p, 4 - k)
        for p in range(PARTS):
            onward(p, 0, 0)
        for p in range(PARTS):
            second[p][2].wait_recv()
            to_neighbours(p, 2)
            over(p, 0)
        fill_two()
        for p in range(PARTS):
            onward(p, 1, 3)
        for p in range(PARTS):
            three[p][0][3].wait_recv()
            three[p][1][0].wait_recv()
            for r in STRAIGHT:
                for way in range(2):
                    three[p][way][r].wait_recv()
            over(p, 1)
            over(p, 3)
        for p in range(PARTS):
            for r, copy in ((0, four[p][0][0]), (1, three[p][2][1]), (3, four[p][1][3]), (2, three[p][2][2])):
                copy.wait_recv()
                across.append(share(p, plane(p, 2, r), other))
        return across

    def nothing():
        pass

    def turn_dec():
        for copy in load_dec:
            copy.wait()

        @pl.loop(0, 2)
        def _(h):
            for q in range(PARTS):
                dec_t[pl.ds(pl.multiple_of(h * HALF + q * GROUP, 128), GROUP), :] = dec[
                    h, :, q * GROUP : (q + 1) * GROUP
                ].T

        norms[...] = jnp.zeros_like(norms)

        @pl.loop(0, 9)
        def _(r):
            rows = dec_t[pl.ds(pl.multiple_of(r * 256, 256), 256), :].astype(jnp.float32)
            norms[...] += jnp.sum(rows * rows, axis=0, keepdims=True)

        norms[...] = jnp.sqrt(norms[...]) * (l1_coeff / loss_norm)

    def wide(buf, t, of_core):
        return jnp.concatenate(
            [buf[of_core * PARTS + p, t].reshape(TILE, GROUP) for p in range(PARTS)], axis=1
        )

    def half_rows(of_core):
        return pl.ds(pl.multiple_of(of_core * HALF, 128), HALF)

    def product(buf, matrix, across, use):
        @pl.loop(0, ROWS // TILE)
        def _(t):
            half_sum[t] = jnp.dot(
                wide(buf, t, core), matrix[half_rows(core), :], preferred_element_type=jnp.float32
            )

        for copy in across:
            copy.wait_recv()
        for t in range(ROWS // TILE):
            use(
                t,
                half_sum[t]
                + jnp.dot(
                    wide(buf, t, 1 - core),
                    matrix[half_rows(1 - core), :],
                    preferred_element_type=jnp.float32,
                ),
            )

    across = gather(cen, [own_cen[p] for p in range(PARTS)], nothing, turn_dec)
    load_weight.wait()
    keep_weight = local(weight, kept_out.at[pl.ds(D, D), pl.ds(LAT_DEV, LAT_DEV)])
    crossing = []

    def encode(t, pre):
        codes[t] = jnp.maximum(pre + enc_bias_in[...], 0.0).astype(jnp.bfloat16)
        made = jnp.dot(codes[t], dec[1 - core], preferred_element_type=jnp.float32)
        for p in range(PARTS):
            cross_send[p, t] = (
                made[:, p * GROUP : (p + 1) * GROUP].astype(jnp.bfloat16).reshape(4, 64, GROUP)
            )
        crossing.append(remote(cross_send.at[:, t], cross_recv.at[:, t], other))

    product(cen, weight, across, encode)

    @pl.loop(0, ROWS // TILE)
    def _(t):
        made = jnp.dot(codes[t], dec[core], preferred_element_type=jnp.float32)
        for p in range(PARTS):
            part_sum[p, t] = made[:, p * GROUP : (p + 1) * GROUP].reshape(4, 64, GROUP)

    for copy in crossing:
        copy.wait_recv()

    def here(p, sel):
        where = (p,) + place(sel)
        value = part_sum[where] + cross_recv[where].astype(jnp.float32)
        return value.reshape(-1, GROUP)

    def turn_centered(first, last):
        @pl.loop(0, ROWS // TILE)
        def _(t):
            for g in range(first, last):
                cen_t[g * GROUP : (g + 1) * GROUP, pl.ds(pl.multiple_of(t * TILE, TILE), TILE)] = (
                    cen[g, t].reshape(TILE, GROUP).T
                )

    step_a = [{} for _ in range(PARTS)]
    step_b = [[{}, {}] for _ in range(PARTS)]

    def to_far(p, r, k):
        a_send[p, r] = here(p, plane(p, 2, r)).astype(jnp.bfloat16)
        step_a[p][r] = remote(a_send.at[p, r], a_recv.at[p, r], peer(ORDER[p][2], k))

    def to_owner(p, way, r):
        k = (1, 3)[way]
        value = here(p, plane(p, k, r))
        if r in ROUTE[way]:
            step_a[p][r].wait_recv()
            value = value + a_recv[p, r].astype(jnp.float32)
        b_send[p, way, r] = value.astype(jnp.bfloat16)
        step_b[p][way][r] = remote(b_send.at[p, way, r], b_recv.at[p, way, r], peer(ORDER[p][2], k))

    for way, k in ((0, 1), (1, 3)):
        for r in ROUTE[way]:
            for p in range(PARTS):
                to_far(p, r, k)
    for r in (2, 1):
        for p in range(PARTS):
            to_far(p, r, 2)
            for way in range(2):
                to_owner(p, way, r)
    for way in range(2):
        for r in ROUTE[1 - way]:
            for p in range(PARTS):
                to_owner(p, way, r)
    for way in range(2):
        for r in ROUTE[way]:
            for p in range(PARTS):
                to_owner(p, way, r)
    turn_centered(0, 4)
    step_c = [{} for _ in range(PARTS)]
    for r in (2, 1, 3, 0):
        for p in range(PARTS):
            value = here(p, plane(p, 0, r))
            if r in STRAIGHT:
                step_a[p][r].wait_recv()
                value = value + a_recv[p, r].astype(jnp.float32)
            for way in range(2):
                step_b[p][way][r].wait_recv()
                value = value + b_recv[p, way, r].astype(jnp.float32)
            c_send[p, r] = value.astype(jnp.bfloat16).reshape(4, BLOCK, GROUP)
            if r == 0:
                plane_sum[p] = value.reshape(4, BLOCK, GROUP)
            for q in (2, 1, 3, 0):
                if q or r:
                    step_c[p][q, r] = remote(
                        c_send.at[p, r, along(ORDER[p][0], q)], c_recv.at[p, r, q], across_plane(p, q, r)
                    )
    kept = []
    for p in range(PARTS):
        value = plane_sum[p, pos[ORDER[p][0]]]
        for r in (2, 1, 3, 0):
            for q in STEPS:
                if q or r:
                    step_c[p][q, r].wait_recv()
                    value = value + c_recv[p, r, q].astype(jnp.float32)
        kept.append((value - own_cen[p].astype(jnp.float32)).astype(jnp.bfloat16))

    put = [keep_weight]

    def last_turn():
        turn_centered(4, 6)
        put.append(local(cen_t, kept_out.at[pl.ds(0, D)]))

    across = gather(err, kept, nothing, last_turn)

    def slope_of(t, back):
        slope = jnp.where(
            codes[t].astype(jnp.float32) > 0.0, back * (2.0 / loss_norm) + norms[...], 0.0
        )
        slopes[t * TILE : (t + 1) * TILE, :] = slope.astype(jnp.bfloat16)
        put.append(
            local(
                slopes.at[pl.ds(t * TILE, TILE)],
                kept_out.at[pl.ds(D + t * TILE, TILE), pl.ds(0, LAT_DEV)],
            )
        )

    product(err, dec_t, across, slope_of)
    row = (m * 32 + lat) * 8
    holder = lax.div(row, 32)
    hx = lax.div(lax.rem(row, 32), BLOCK) * 2 + lax.rem(holder, 2)
    hyz = lax.div(holder, 2)
    hz = pl.ds(pl.multiple_of(lax.rem(hyz, 4) * BLOCK, BLOCK), BLOCK)
    upper = lax.rem(row, BLOCK) > 0
    for g in range(2 * PARTS):
        rows = err[g, hx, lax.div(hyz, 4), hz, :].astype(jnp.float32)
        rows = jnp.where(upper, rows[8:], rows[:8])
        error_rows[:, g * GROUP : (g + 1) * GROUP] = jnp.concatenate([rows, rows]).astype(jnp.bfloat16)
    for i in range(3):
        put.append(
            local(
                error_rows.at[:, pl.ds(i * 768, 768)],
                kept_out.at[pl.ds(2 * D + i * BLOCK, BLOCK), pl.ds(0, 768)],
            )
        )
    for copy in put:
        copy.wait()
    for copy in sent:
        copy.wait_send()


N_REMOTE = 3 + 2 * PARTS * (6 + 10 + 2 + 7) + 4 + PARTS * (4 + 8 + 15)
N_LOCAL = 4 + 2 + 1 + 1 + 1 + 4 + 3
KEPT = 8192


def exchange(resid, terms, dec_bias, enc_weight, enc_bias, dec_weight):
    bf16, f32 = jnp.bfloat16, jnp.float32
    anywhere = pl.BlockSpec(memory_space=pl.ANY)
    hbm = pl.BlockSpec(memory_space=pltpu.HBM)
    return pl.pallas_call(
        exchange_kernel,
        out_shape=jax.ShapeDtypeStruct((KEPT, ROWS), bf16),
        in_specs=[hbm] * 6,
        out_specs=anywhere,
        scratch_shapes=[
            pltpu.VMEM((6, 4, 4, 64, GROUP), bf16),
            pltpu.VMEM((6, 4, 4, 64, GROUP), bf16),
            pltpu.VMEM((D, ROWS), bf16),
            pltpu.VMEM((D, LAT_DEV), bf16),
            pltpu.VMEM((2, LAT_DEV, HALF), bf16),
            pltpu.VMEM((D, LAT_DEV), bf16),
            pltpu.VMEM((1, LAT_DEV), f32),
            pltpu.VMEM((4, TILE, LAT_DEV), bf16),
            pltpu.VMEM((PARTS, 4, 4, 64, GROUP), bf16),
            pltpu.VMEM((PARTS, 4, 4, 64, GROUP), bf16),
            pltpu.VMEM((PARTS, 4, 4, 64, GROUP), f32),
            pltpu.VMEM((PARTS, 4, 64, GROUP), bf16),
            pltpu.VMEM((PARTS, 4, 64, GROUP), bf16),
            pltpu.VMEM((PARTS, 2, 4, 64, GROUP), bf16),
            pltpu.VMEM((PARTS, 2, 4, 64, GROUP), bf16),
            pltpu.VMEM((PARTS, 4, 4, BLOCK, GROUP), bf16),
            pltpu.VMEM((PARTS, 4, 4, BLOCK, GROUP), bf16),
            pltpu.VMEM((PARTS, 4, BLOCK, GROUP), f32),
            pltpu.VMEM((ROWS, LAT_DEV), bf16),
            pltpu.VMEM((4, TILE, LAT_DEV), f32),
            pltpu.VMEM((4, BLOCK, HALF), bf16),
            pltpu.VMEM((BLOCK, HALF), bf16),
            pltpu.VMEM((D,), f32),
            pltpu.VMEM((1, LAT_DEV), f32),
            pltpu.VMEM((PARTS, BLOCK, GROUP), bf16),
            pltpu.VMEM((BLOCK, D), bf16),
            pltpu.SemaphoreType.DMA((N_REMOTE,)),
            pltpu.SemaphoreType.DMA((N_REMOTE,)),
            pltpu.SemaphoreType.DMA((N_LOCAL,)),
        ],
        cost_estimate=pl.CostEstimate(flops=90_000_000_000, bytes_accessed=10_000_000, transcendentals=0),
        compiler_params=pltpu.CompilerParams(
            collective_id=0, has_side_effects=True, vmem_limit_bytes=54 * 1024 * 1024
        ),
    )(resid, terms, dec_bias, enc_weight, enc_bias, dec_weight)


TILES = D // TILE


def adam_kernel(
    kept, first, second,
    weight_new, first_new, second_new, error_new,
    cen_in, slopes_in, weight_in, one_in, two_in, error_in, weight_out, one_out, two_out,
    in_sems, out_sems, lone_sems,
):
    def tile(t):
        return pl.ds(t * TILE, TILE)

    load_slopes = pltpu.make_async_copy(
        kept.at[pl.ds(D, ROWS), pl.ds(0, LAT_DEV)], slopes_in, lone_sems.at[0]
    )
    load_slopes.start()
    loads = []
    for t in range(TILES):
        pairs = (
            (kept.at[tile(t)], cen_in),
            (kept.at[pl.ds(D + t * TILE, TILE), pl.ds(LAT_DEV, LAT_DEV)], weight_in),
            (first.at[tile(t)], one_in),
            (second.at[tile(t)], two_in),
        )
        step = [
            pltpu.make_async_copy(src, dst.at[tile(t)], in_sems.at[i, t])
            for i, (src, dst) in enumerate(pairs)
        ]
        for copy in step:
            copy.start()
        loads.append(step)
    load_error = [
        pltpu.make_async_copy(
            kept.at[pl.ds(2 * D + i * BLOCK, BLOCK), pl.ds(0, 768)],
            error_in.at[:, pl.ds(i * 768, 768)],
            lone_sems.at[1 + i],
        )
        for i in range(3)
    ]
    for copy in load_error:
        copy.start()
    load_slopes.wait()
    corr_one = 1.0 - beta_one**STEP
    corr_two = 1.0 - beta_two**STEP
    stores = []
    for t in range(TILES):
        for copy in loads[t]:
            copy.wait()
        rows = tile(t)
        grad = jnp.dot(cen_in[rows], slopes_in[...], preferred_element_type=jnp.float32)
        one = beta_one * one_in[rows] + (1.0 - beta_one) * grad
        two = beta_two * two_in[rows] + (1.0 - beta_two) * grad * grad
        one_out[rows] = one
        two_out[rows] = two
        scaled = two * (1.0 / corr_two)
        change = one * (learn_rate / corr_one) / (scaled * lax.rsqrt(scaled) + adam_eps)
        weight_out[rows] = (weight_in[rows].astype(jnp.float32) - change).astype(jnp.bfloat16)
        pairs = ((one_out, first_new), (two_out, second_new), (weight_out, weight_new))
        for i, (src, dst) in enumerate(pairs):
            copy = pltpu.make_async_copy(src.at[rows], dst.at[rows], out_sems.at[i, t])
            copy.start()
            stores.append(copy)
    for copy in load_error:
        copy.wait()
    error_new[...] = error_in[:8, :]
    for copy in stores:
        copy.wait()


def adam(kept, first, second):
    bf16, f32 = jnp.bfloat16, jnp.float32
    anywhere = pl.BlockSpec(memory_space=pl.ANY)
    hbm = pl.BlockSpec(memory_space=pltpu.HBM)
    return pl.pallas_call(
        adam_kernel,
        out_shape=(
            jax.ShapeDtypeStruct((D, LAT_DEV), bf16),
            jax.ShapeDtypeStruct((D, LAT_DEV), f32),
            jax.ShapeDtypeStruct((D, LAT_DEV), f32),
            jax.ShapeDtypeStruct((8, D), bf16),
        ),
        in_specs=[anywhere] * 3,
        out_specs=(hbm, hbm, hbm, pl.BlockSpec(memory_space=pltpu.VMEM)),
        scratch_shapes=[
            pltpu.VMEM((D, ROWS), bf16),
            pltpu.VMEM((ROWS, LAT_DEV), bf16),
            pltpu.VMEM((D, LAT_DEV), bf16),
            pltpu.VMEM((D, LAT_DEV), f32),
            pltpu.VMEM((D, LAT_DEV), f32),
            pltpu.VMEM((BLOCK, D), bf16),
            pltpu.VMEM((D, LAT_DEV), bf16),
            pltpu.VMEM((D, LAT_DEV), f32),
            pltpu.VMEM((D, LAT_DEV), f32),
            pltpu.SemaphoreType.DMA((4, TILES)),
            pltpu.SemaphoreType.DMA((3, TILES)),
            pltpu.SemaphoreType.DMA((4,)),
        ],
        cost_estimate=pl.CostEstimate(
            flops=2 * ROWS * D * LAT_DEV, bytes_accessed=29_000_000, transcendentals=0
        ),
        compiler_params=pltpu.CompilerParams(vmem_limit_bytes=44 * 1024 * 1024),
    )(kept, first, second)


def on_device(
    resid_in, layer_terms, dec_bias, enc_weight, enc_bias, dec_weight, first_moment, second_moment
):
    kept = exchange(
        resid_in, layer_terms, dec_bias, enc_weight, enc_bias[None], dec_weight
    )
    return adam(kept, first_moment, second_moment)


def solution(mesh):
    in_specs = (
        P("lat", None),
        P("mp", "lat", None),
        P(),
        P(None, ("mp", "lat")),
        P(("mp", "lat")),
        P(("mp", "lat"), None),
        P(None, ("mp", "lat")),
        P(None, ("mp", "lat")),
    )
    out_specs = (
        P(None, ("mp", "lat")),
        P(None, ("mp", "lat")),
        P(None, ("mp", "lat")),
        P(("mp", "lat"), None),
    )
    return jax.shard_map(
        on_device, mesh=mesh, in_specs=in_specs, out_specs=out_specs, check_vma=False
    )
```

```python
import jax
import jax.numpy as jnp
from jax import lax
from jax.experimental import pallas as pl
from jax.experimental.pallas import tpu as pltpu
from jax.sharding import PartitionSpec as P

MESH = pl.DeviceIdType.MESH
STEP = 10
l1_coeff = 5.0
loss_norm = 32.0
beta_one = 0.9
beta_two = 0.95
learn_rate = 0.001
adam_eps = 1e-08

D = 2304
HALF = D // 2
GROUP = HALF // 3
PARTS = 3
LAT_DEV = 512
ROWS = 1024
BLOCK = 16
TILE = 256
ORDER = ((2, 1, 0), (0, 2, 1), (1, 0, 2))


def exchange_kernel(
    resid, terms, dec_bias, enc_weight, enc_bias, dec_weight,
    kept_out,
    cen, err, cen_t, weight, dec, dec_t, norms, codes, cross_send, cross_recv, part_sum,
    a_send, a_recv, b_send, b_recv, c_send, c_recv, plane_sum, slopes, half_sum,
    term_in, resid_in, bias_in, enc_bias_in, own_cen, error_rows,
    send_sems, recv_sems, local_sems, ready,
):
    m = lax.axis_index("mp")
    lat = lax.axis_index("lat")
    core = lax.rem(m, 2)
    yz = lax.div(lat, 2)
    x = lax.div(m, 2) * 2 + lax.rem(lat, 2)
    pos = (x, lax.div(yz, 4), lax.rem(yz, 4))

    def device(at, on_core):
        return (lax.div(at[0], 2) * 2 + on_core, (at[1] * 4 + at[2]) * 2 + lax.rem(at[0], 2))

    def along(axis, k):
        return lax.rem(pos[axis] + k, 4)

    def peer(axis, k):
        at = list(pos)
        at[axis] = along(axis, k)
        return device(at, core)

    other = device(pos, 1 - core)
    g0 = core * PARTS

    count = [0, 0]
    sent = []

    def remote(src, dst, to):
        i = count[0]
        count[0] += 1
        copy = pltpu.make_async_remote_copy(
            src_ref=src, dst_ref=dst, send_sem=send_sems.at[i], recv_sem=recv_sems.at[i],
            device_id=to, device_id_type=MESH,
        )
        copy.start()
        sent.append(copy)
        return copy

    def local(src, dst):
        i = count[1]
        count[1] += 1
        copy = pltpu.make_async_copy(src, dst, local_sems.at[i])
        copy.start()
        return copy

    rows16 = pl.ds(pl.multiple_of(lax.div(m, 2) * BLOCK, BLOCK), BLOCK)
    half = pl.ds(pl.multiple_of(core * HALF, 128), HALF)
    early = [
        local(terms.at[0, rows16, half], term_in.at[0]),
        local(resid.at[rows16, half], resid_in),
        local(dec_bias, bias_in),
        local(enc_bias, enc_bias_in),
    ]
    load_dec = [local(dec_weight.at[:, pl.ds(h * HALF, HALF)], dec.at[h]) for h in range(2)]
    load_weight = local(enc_weight, weight)

    barrier = pltpu.get_barrier_semaphore()
    greet = [other, device((lax.rem(x + 2, 4), pos[1], pos[2]), 1 - core)]
    greet += [peer(axis, k) for axis in range(3) for k in (1, 2, 3)]
    for to in greet:
        pl.semaphore_signal(barrier, inc=1, device_id=to, device_id_type=MESH)
    pl.semaphore_wait(barrier, len(greet))
    for to in greet[2:]:
        pl.semaphore_signal(ready, inc=1, device_id=to, device_id_type=MESH)

    moves = []
    for k in (1, 2, 3):
        mt = lax.rem(m + k, 4)
        moves.append(
            remote(
                terms.at[
                    0,
                    pl.ds(pl.multiple_of(lax.div(mt, 2) * BLOCK, BLOCK), BLOCK),
                    pl.ds(pl.multiple_of(lax.rem(mt, 2) * HALF, 128), HALF),
                ],
                term_in.at[k],
                (mt, lat),
            )
        )
    for copy in early:
        copy.wait()
    for copy in moves:
        copy.wait_recv()
    total = term_in[0].astype(jnp.float32)
    for k in (1, 2, 3):
        total = total + term_in[k].astype(jnp.float32)
    bias = bias_in[...].reshape(1, D)
    bias = jnp.where(core == 0, bias[:, :HALF], bias[:, HALF:])
    own = (resid_in[...].astype(jnp.float32) + total - bias).astype(jnp.bfloat16)
    for p in range(PARTS):
        own_cen[p] = own[:, p * GROUP : (p + 1) * GROUP]

    def place(sel):
        return (
            pl.ds(*sel[0]),
            pl.ds(*sel[1]),
            pl.ds(pl.multiple_of(sel[2][0] * BLOCK, BLOCK), sel[2][1] * BLOCK),
        )

    def only(base, axis, start, size):
        sel = list(base)
        sel[axis] = (start, size)
        return sel

    own_sel = [(pos[0], 1), (pos[1], 1), (pos[2], 1)]
    full = [(0, 4), (0, 4), (0, 4)]
    ROUTE = ((0,), (3,))
    STRAIGHT = (1, 2)
    STEPS = (0, 1, 3, 2)

    def plane(p, k_last, k_second):
        sel = only(full, ORDER[p][2], along(ORDER[p][2], k_last), 1)
        return only(sel, ORDER[p][1], along(ORDER[p][1], k_second), 1)

    def across_plane(p, q, r):
        at = list(pos)
        at[ORDER[p][0]] = along(ORDER[p][0], q)
        at[ORDER[p][1]] = along(ORDER[p][1], r)
        return device(at, core)

    def gather(buf, blocks, fill_one, fill_two):
        def at(p, sel):
            return buf.at[(g0 + p,) + place(sel)]

        def share(p, sel, to):
            return remote(at(p, sel), at(p, sel), to)

        for p in range(PARTS):
            buf[(g0 + p,) + place(own_sel)] = blocks[p][None, None]
        across = []
        first = [{} for _ in range(PARTS)]
        three = [[{}, {}, {}] for _ in range(PARTS)]
        four = [[{}, {}] for _ in range(PARTS)]

        def arrived(p, r):
            for q in STEPS:
                if q or r:
                    first[p][q, (4 - r) % 4].wait_recv()

        def to_neighbours(p, r):
            for way, k in ((0, 1), (1, 3)):
                three[p][way][r] = share(p, plane(p, 0, r), peer(ORDER[p][2], k))
            if r in STRAIGHT:
                three[p][2][r] = share(p, plane(p, 0, r), peer(ORDER[p][2], 2))

        def onward(p, way, r):
            k = (1, 3)[way]
            three[p][way][r].wait_recv()
            four[p][way][r] = share(p, plane(p, 4 - k, r), peer(ORDER[p][2], k))

        def over(p, k):
            sel = only(full, ORDER[p][2], along(ORDER[p][2], k), 1)
            across.append(share(p, sel, other))

        for r in STEPS:
            for p in range(PARTS):
                for q in STEPS:
                    if q or r:
                        first[p][q, r] = share(p, own_sel, across_plane(p, q, r))
        fill_one()
        for r in (0, 3, 1):
            for p in range(PARTS):
                arrived(p, r)
                to_neighbours(p, r)
        for p in range(PARTS):
            onward(p, 0, 0)
        for p in range(PARTS):
            arrived(p, 2)
            to_neighbours(p, 2)
            over(p, 0)
        fill_two()
        for p in range(PARTS):
            onward(p, 1, 3)
        for p in range(PARTS):
            three[p][0][3].wait_recv()
            three[p][1][0].wait_recv()
            for r in STRAIGHT:
                for way in range(2):
                    three[p][way][r].wait_recv()
            over(p, 1)
            over(p, 3)
        for p in range(PARTS):
            for r, copy in ((0, four[p][0][0]), (1, three[p][2][1]), (3, four[p][1][3]), (2, three[p][2][2])):
                copy.wait_recv()
                across.append(share(p, plane(p, 2, r), other))
        return across

    def nothing():
        pass

    def turn_dec():
        for copy in load_dec:
            copy.wait()

        @pl.loop(0, 2)
        def _(h):
            for q in range(PARTS):
                dec_t[pl.ds(pl.multiple_of(h * HALF + q * GROUP, 128), GROUP), :] = dec[
                    h, :, q * GROUP : (q + 1) * GROUP
                ].T

        norms[...] = jnp.zeros_like(norms)

        @pl.loop(0, 9)
        def _(r):
            rows = dec_t[pl.ds(pl.multiple_of(r * 256, 256), 256), :].astype(jnp.float32)
            norms[...] += jnp.sum(rows * rows, axis=0, keepdims=True)

        norms[...] = jnp.sqrt(norms[...]) * (l1_coeff / loss_norm)

    def wide(buf, t, of_core):
        return jnp.concatenate(
            [buf[of_core * PARTS + p, t].reshape(TILE, GROUP) for p in range(PARTS)], axis=1
        )

    def half_rows(of_core):
        return pl.ds(pl.multiple_of(of_core * HALF, 128), HALF)

    def product(buf, matrix, across, use):
        @pl.loop(0, ROWS // TILE)
        def _(t):
            half_sum[t] = jnp.dot(
                wide(buf, t, core), matrix[half_rows(core), :], preferred_element_type=jnp.float32
            )

        for copy in across:
            copy.wait_recv()
        for t in range(ROWS // TILE):
            use(
                t,
                half_sum[t]
                + jnp.dot(
                    wide(buf, t, 1 - core),
                    matrix[half_rows(1 - core), :],
                    preferred_element_type=jnp.float32,
                ),
            )

    pl.semaphore_wait(ready, len(greet) - 2)
    across = gather(cen, [own_cen[p] for p in range(PARTS)], nothing, turn_dec)
    load_weight.wait()
    keep_weight = local(weight, kept_out.at[pl.ds(D, D), pl.ds(LAT_DEV, LAT_DEV)])
    crossing = []

    def encode(t, pre):
        codes[t] = jnp.maximum(pre + enc_bias_in[...], 0.0).astype(jnp.bfloat16)
        made = jnp.dot(codes[t], dec[1 - core], preferred_element_type=jnp.float32)
        for p in range(PARTS):
            cross_send[p, t] = (
                made[:, p * GROUP : (p + 1) * GROUP].astype(jnp.bfloat16).reshape(4, 64, GROUP)
            )
        crossing.append(remote(cross_send.at[:, t], cross_recv.at[:, t], other))

    product(cen, weight, across, encode)

    @pl.loop(0, ROWS // TILE)
    def _(t):
        made = jnp.dot(codes[t], dec[core], preferred_element_type=jnp.float32)
        for p in range(PARTS):
            part_sum[p, t] = made[:, p * GROUP : (p + 1) * GROUP].reshape(4, 64, GROUP)

    for copy in crossing:
        copy.wait_recv()

    def here(p, sel):
        where = (p,) + place(sel)
        value = part_sum[where] + cross_recv[where].astype(jnp.float32)
        return value.reshape(-1, GROUP)

    def turn_centered(first, last):
        @pl.loop(0, ROWS // TILE)
        def _(t):
            for g in range(first, last):
                cen_t[g * GROUP : (g + 1) * GROUP, pl.ds(pl.multiple_of(t * TILE, TILE), TILE)] = (
                    cen[g, t].reshape(TILE, GROUP).T
                )

    step_a = [{} for _ in range(PARTS)]
    step_b = [[{}, {}] for _ in range(PARTS)]

    def to_far(p, r, k):
        a_send[p, r] = here(p, plane(p, 2, r)).astype(jnp.bfloat16)
        step_a[p][r] = remote(a_send.at[p, r], a_recv.at[p, r], peer(ORDER[p][2], k))

    def to_owner(p, way, r):
        k = (1, 3)[way]
        value = here(p, plane(p, k, r))
        if r in ROUTE[way]:
            step_a[p][r].wait_recv()
            value = value + a_recv[p, r].astype(jnp.float32)
        b_send[p, way, r] = value.astype(jnp.bfloat16)
        step_b[p][way][r] = remote(b_send.at[p, way, r], b_recv.at[p, way, r], peer(ORDER[p][2], k))

    for way, k in ((0, 1), (1, 3)):
        for r in ROUTE[way]:
            for p in range(PARTS):
                to_far(p, r, k)
    for r in (2, 1):
        for p in range(PARTS):
            to_far(p, r, 2)
            for way in range(2):
                to_owner(p, way, r)
    for way in range(2):
        for r in ROUTE[1 - way]:
            for p in range(PARTS):
                to_owner(p, way, r)
    for way in range(2):
        for r in ROUTE[way]:
            for p in range(PARTS):
                to_owner(p, way, r)
    turn_centered(0, 4)
    step_c = [{} for _ in range(PARTS)]
    for r in (2, 1, 3, 0):
        for p in range(PARTS):
            value = here(p, plane(p, 0, r))
            if r in STRAIGHT:
                step_a[p][r].wait_recv()
                value = value + a_recv[p, r].astype(jnp.float32)
            for way in range(2):
                step_b[p][way][r].wait_recv()
                value = value + b_recv[p, way, r].astype(jnp.float32)
            c_send[p, r] = value.astype(jnp.bfloat16).reshape(4, BLOCK, GROUP)
            if r == 0:
                plane_sum[p] = value.reshape(4, BLOCK, GROUP)
            for q in (2, 1, 3, 0):
                if q or r:
                    step_c[p][q, r] = remote(
                        c_send.at[p, r, along(ORDER[p][0], q)], c_recv.at[p, r, q], across_plane(p, q, r)
                    )
    kept = []
    for p in range(PARTS):
        value = plane_sum[p, pos[ORDER[p][0]]]
        for r in (2, 1, 3, 0):
            for q in STEPS:
                if q or r:
                    step_c[p][q, r].wait_recv()
                    value = value + c_recv[p, r, q].astype(jnp.float32)
        kept.append((value - own_cen[p].astype(jnp.float32)).astype(jnp.bfloat16))

    put = [keep_weight]

    def last_turn():
        turn_centered(4, 6)
        put.append(local(cen_t, kept_out.at[pl.ds(0, D)]))

    across = gather(err, kept, nothing, last_turn)

    def slope_of(t, back):
        slope = jnp.where(
            codes[t].astype(jnp.float32) > 0.0, back * (2.0 / loss_norm) + norms[...], 0.0
        )
        slopes[t * TILE : (t + 1) * TILE, :] = slope.astype(jnp.bfloat16)
        put.append(
            local(
                slopes.at[pl.ds(t * TILE, TILE)],
                kept_out.at[pl.ds(D + t * TILE, TILE), pl.ds(0, LAT_DEV)],
            )
        )

    product(err, dec_t, across, slope_of)
    row = (m * 32 + lat) * 8
    holder = lax.div(row, 32)
    hx = lax.div(lax.rem(row, 32), BLOCK) * 2 + lax.rem(holder, 2)
    hyz = lax.div(holder, 2)
    hz = pl.ds(pl.multiple_of(lax.rem(hyz, 4) * BLOCK, BLOCK), BLOCK)
    upper = lax.rem(row, BLOCK) > 0
    for g in range(2 * PARTS):
        rows = err[g, hx, lax.div(hyz, 4), hz, :].astype(jnp.float32)
        rows = jnp.where(upper, rows[8:], rows[:8])
        error_rows[:, g * GROUP : (g + 1) * GROUP] = jnp.concatenate([rows, rows]).astype(jnp.bfloat16)
    for i in range(3):
        put.append(
            local(
                error_rows.at[:, pl.ds(i * 768, 768)],
                kept_out.at[pl.ds(2 * D + i * BLOCK, BLOCK), pl.ds(0, 768)],
            )
        )
    for copy in put:
        copy.wait()
    for copy in sent:
        copy.wait_send()


N_REMOTE = 3 + 2 * PARTS * (15 + 10 + 2 + 7) + 4 + PARTS * (4 + 8 + 15)
N_LOCAL = 4 + 2 + 1 + 1 + 1 + 4 + 3
KEPT = 8192


def exchange(resid, terms, dec_bias, enc_weight, enc_bias, dec_weight):
    bf16, f32 = jnp.bfloat16, jnp.float32
    anywhere = pl.BlockSpec(memory_space=pl.ANY)
    hbm = pl.BlockSpec(memory_space=pltpu.HBM)
    return pl.pallas_call(
        exchange_kernel,
        out_shape=jax.ShapeDtypeStruct((KEPT, ROWS), bf16),
        in_specs=[hbm] * 6,
        out_specs=anywhere,
        scratch_shapes=[
            pltpu.VMEM((6, 4, 4, 64, GROUP), bf16),
            pltpu.VMEM((6, 4, 4, 64, GROUP), bf16),
            pltpu.VMEM((D, ROWS), bf16),
            pltpu.VMEM((D, LAT_DEV), bf16),
            pltpu.VMEM((2, LAT_DEV, HALF), bf16),
            pltpu.VMEM((D, LAT_DEV), bf16),
            pltpu.VMEM((1, LAT_DEV), f32),
            pltpu.VMEM((4, TILE, LAT_DEV), bf16),
            pltpu.VMEM((PARTS, 4, 4, 64, GROUP), bf16),
            pltpu.VMEM((PARTS, 4, 4, 64, GROUP), bf16),
            pltpu.VMEM((PARTS, 4, 4, 64, GROUP), f32),
            pltpu.VMEM((PARTS, 4, 64, GROUP), bf16),
            pltpu.VMEM((PARTS, 4, 64, GROUP), bf16),
            pltpu.VMEM((PARTS, 2, 4, 64, GROUP), bf16),
            pltpu.VMEM((PARTS, 2, 4, 64, GROUP), bf16),
            pltpu.VMEM((PARTS, 4, 4, BLOCK, GROUP), bf16),
            pltpu.VMEM((PARTS, 4, 4, BLOCK, GROUP), bf16),
            pltpu.VMEM((PARTS, 4, BLOCK, GROUP), f32),
            pltpu.VMEM((ROWS, LAT_DEV), bf16),
            pltpu.VMEM((4, TILE, LAT_DEV), f32),
            pltpu.VMEM((4, BLOCK, HALF), bf16),
            pltpu.VMEM((BLOCK, HALF), bf16),
            pltpu.VMEM((D,), f32),
            pltpu.VMEM((1, LAT_DEV), f32),
            pltpu.VMEM((PARTS, BLOCK, GROUP), bf16),
            pltpu.VMEM((BLOCK, D), bf16),
            pltpu.SemaphoreType.DMA((N_REMOTE,)),
            pltpu.SemaphoreType.DMA((N_REMOTE,)),
            pltpu.SemaphoreType.DMA((N_LOCAL,)),
            pltpu.SemaphoreType.REGULAR,
        ],
        cost_estimate=pl.CostEstimate(flops=90_000_000_000, bytes_accessed=10_000_000, transcendentals=0),
        compiler_params=pltpu.CompilerParams(
            collective_id=0, has_side_effects=True, vmem_limit_bytes=54 * 1024 * 1024
        ),
    )(resid, terms, dec_bias, enc_weight, enc_bias, dec_weight)


TILES = D // TILE


def adam_kernel(
    kept, first, second,
    weight_new, first_new, second_new, error_new,
    cen_in, slopes_in, weight_in, one_in, two_in, error_in, weight_out, one_out, two_out,
    in_sems, out_sems, lone_sems,
):
    def tile(t):
        return pl.ds(t * TILE, TILE)

    load_slopes = pltpu.make_async_copy(
        kept.at[pl.ds(D, ROWS), pl.ds(0, LAT_DEV)], slopes_in, lone_sems.at[0]
    )
    load_slopes.start()
    loads = []
    for t in range(TILES):
        pairs = (
            (kept.at[tile(t)], cen_in),
            (kept.at[pl.ds(D + t * TILE, TILE), pl.ds(LAT_DEV, LAT_DEV)], weight_in),
            (first.at[tile(t)], one_in),
            (second.at[tile(t)], two_in),
        )
        step = [
            pltpu.make_async_copy(src, dst.at[tile(t)], in_sems.at[i, t])
            for i, (src, dst) in enumerate(pairs)
        ]
        for copy in step:
            copy.start()
        loads.append(step)
    load_error = [
        pltpu.make_async_copy(
            kept.at[pl.ds(2 * D + i * BLOCK, BLOCK), pl.ds(0, 768)],
            error_in.at[:, pl.ds(i * 768, 768)],
            lone_sems.at[1 + i],
        )
        for i in range(3)
    ]
    for copy in load_error:
        copy.start()
    load_slopes.wait()
    corr_one = 1.0 - beta_one**STEP
    corr_two = 1.0 - beta_two**STEP
    stores = []
    for t in range(TILES):
        for copy in loads[t]:
            copy.wait()
        rows = tile(t)
        grad = jnp.dot(cen_in[rows], slopes_in[...], preferred_element_type=jnp.float32)
        one = beta_one * one_in[rows] + (1.0 - beta_one) * grad
        two = beta_two * two_in[rows] + (1.0 - beta_two) * grad * grad
        one_out[rows] = one
        two_out[rows] = two
        scaled = two * (1.0 / corr_two)
        change = one * (learn_rate / corr_one) / (scaled * lax.rsqrt(scaled) + adam_eps)
        weight_out[rows] = (weight_in[rows].astype(jnp.float32) - change).astype(jnp.bfloat16)
        pairs = ((one_out, first_new), (two_out, second_new), (weight_out, weight_new))
        for i, (src, dst) in enumerate(pairs):
            copy = pltpu.make_async_copy(src.at[rows], dst.at[rows], out_sems.at[i, t])
            copy.start()
            stores.append(copy)
    for copy in load_error:
        copy.wait()
    error_new[...] = error_in[:8, :]
    for copy in stores:
        copy.wait()


def adam(kept, first, second):
    bf16, f32 = jnp.bfloat16, jnp.float32
    anywhere = pl.BlockSpec(memory_space=pl.ANY)
    hbm = pl.BlockSpec(memory_space=pltpu.HBM)
    return pl.pallas_call(
        adam_kernel,
        out_shape=(
            jax.ShapeDtypeStruct((D, LAT_DEV), bf16),
            jax.ShapeDtypeStruct((D, LAT_DEV), f32),
            jax.ShapeDtypeStruct((D, LAT_DEV), f32),
            jax.ShapeDtypeStruct((8, D), bf16),
        ),
        in_specs=[anywhere] * 3,
        out_specs=(hbm, hbm, hbm, pl.BlockSpec(memory_space=pltpu.VMEM)),
        scratch_shapes=[
            pltpu.VMEM((D, ROWS), bf16),
            pltpu.VMEM((ROWS, LAT_DEV), bf16),
            pltpu.VMEM((D, LAT_DEV), bf16),
            pltpu.VMEM((D, LAT_DEV), f32),
            pltpu.VMEM((D, LAT_DEV), f32),
            pltpu.VMEM((BLOCK, D), bf16),
            pltpu.VMEM((D, LAT_DEV), bf16),
            pltpu.VMEM((D, LAT_DEV), f32),
            pltpu.VMEM((D, LAT_DEV), f32),
            pltpu.SemaphoreType.DMA((4, TILES)),
            pltpu.SemaphoreType.DMA((3, TILES)),
            pltpu.SemaphoreType.DMA((4,)),
        ],
        cost_estimate=pl.CostEstimate(
            flops=2 * ROWS * D * LAT_DEV, bytes_accessed=29_000_000, transcendentals=0
        ),
        compiler_params=pltpu.CompilerParams(vmem_limit_bytes=44 * 1024 * 1024),
    )(kept, first, second)


def on_device(
    resid_in, layer_terms, dec_bias, enc_weight, enc_bias, dec_weight, first_moment, second_moment
):
    kept = exchange(
        resid_in, layer_terms, dec_bias, enc_weight, enc_bias[None], dec_weight
    )
    return adam(kept, first_moment, second_moment)


def solution(mesh):
    in_specs = (
        P("lat", None),
        P("mp", "lat", None),
        P(),
        P(None, ("mp", "lat")),
        P(("mp", "lat")),
        P(("mp", "lat"), None),
        P(None, ("mp", "lat")),
        P(None, ("mp", "lat")),
    )
    out_specs = (
        P(None, ("mp", "lat")),
        P(None, ("mp", "lat")),
        P(None, ("mp", "lat")),
        P(("mp", "lat"), None),
    )
    return jax.shard_map(
        on_device, mesh=mesh, in_specs=in_specs, out_specs=out_specs, check_vma=False
    )
```

```python
import jax
import jax.numpy as jnp
from jax import lax
from jax.experimental import pallas as pl
from jax.experimental.pallas import tpu as pltpu
from jax.sharding import PartitionSpec as P

MESH = pl.DeviceIdType.MESH
STEP = 10
l1_coeff = 5.0
loss_norm = 32.0
beta_one = 0.9
beta_two = 0.95
learn_rate = 0.001
adam_eps = 1e-08

D = 2304
HALF = D // 2
GROUP = HALF // 3
PARTS = 3
LAT_DEV = 512
ROWS = 1024
BLOCK = 16
TILE = 256
ORDER = ((2, 1, 0), (0, 2, 1), (1, 0, 2))


def exchange_kernel(
    resid, terms, dec_bias, enc_weight, enc_bias, dec_weight,
    kept_out,
    cen, err, cen_t, weight, dec, dec_t, norms, codes, cross_send, cross_recv, part_sum,
    a_send, a_recv, b_send, b_recv, c_send, c_recv, plane_sum, slopes, half_sum,
    term_in, resid_in, bias_in, enc_bias_in, own_cen, error_rows,
    send_sems, recv_sems, local_sems, ready,
):
    m = lax.axis_index("mp")
    lat = lax.axis_index("lat")
    core = lax.rem(m, 2)
    yz = lax.div(lat, 2)
    x = lax.div(m, 2) * 2 + lax.rem(lat, 2)
    pos = (x, lax.div(yz, 4), lax.rem(yz, 4))

    def device(at, on_core):
        return (lax.div(at[0], 2) * 2 + on_core, (at[1] * 4 + at[2]) * 2 + lax.rem(at[0], 2))

    def along(axis, k):
        return lax.rem(pos[axis] + k, 4)

    def peer(axis, k):
        at = list(pos)
        at[axis] = along(axis, k)
        return device(at, core)

    other = device(pos, 1 - core)
    g0 = core * PARTS

    count = [0, 0]
    sent = []

    def remote(src, dst, to):
        i = count[0]
        count[0] += 1
        copy = pltpu.make_async_remote_copy(
            src_ref=src, dst_ref=dst, send_sem=send_sems.at[i], recv_sem=recv_sems.at[i],
            device_id=to, device_id_type=MESH,
        )
        copy.start()
        sent.append(copy)
        return copy

    def local(src, dst):
        i = count[1]
        count[1] += 1
        copy = pltpu.make_async_copy(src, dst, local_sems.at[i])
        copy.start()
        return copy

    rows16 = pl.ds(pl.multiple_of(lax.div(m, 2) * BLOCK, BLOCK), BLOCK)
    half = pl.ds(pl.multiple_of(core * HALF, 128), HALF)
    early = [
        local(terms.at[0, rows16, half], term_in.at[0]),
        local(resid.at[rows16, half], resid_in),
        local(dec_bias, bias_in),
        local(enc_bias, enc_bias_in),
    ]
    load_dec = [local(dec_weight.at[:, pl.ds(h * HALF, HALF)], dec.at[h]) for h in range(2)]
    load_weight = local(enc_weight, weight)

    barrier = pltpu.get_barrier_semaphore()
    greet = [other, device((lax.rem(x + 2, 4), pos[1], pos[2]), 1 - core)]
    greet += [peer(axis, k) for axis in range(3) for k in (1, 2, 3)]
    for to in greet:
        pl.semaphore_signal(barrier, inc=1, device_id=to, device_id_type=MESH)
    pl.semaphore_wait(barrier, len(greet))
    for to in greet[2:]:
        pl.semaphore_signal(ready, inc=1, device_id=to, device_id_type=MESH)

    moves = []
    for k in (1, 2, 3):
        mt = lax.rem(m + k, 4)
        moves.append(
            remote(
                terms.at[
                    0,
                    pl.ds(pl.multiple_of(lax.div(mt, 2) * BLOCK, BLOCK), BLOCK),
                    pl.ds(pl.multiple_of(lax.rem(mt, 2) * HALF, 128), HALF),
                ],
                term_in.at[k],
                (mt, lat),
            )
        )
    for copy in early:
        copy.wait()
    for copy in moves:
        copy.wait_recv()
    total = term_in[0].astype(jnp.float32)
    for k in (1, 2, 3):
        total = total + term_in[k].astype(jnp.float32)
    bias = bias_in[...].reshape(1, D)
    bias = jnp.where(core == 0, bias[:, :HALF], bias[:, HALF:])
    own = (resid_in[...].astype(jnp.float32) + total - bias).astype(jnp.bfloat16)
    for p in range(PARTS):
        own_cen[p] = own[:, p * GROUP : (p + 1) * GROUP]

    def place(sel):
        return (
            pl.ds(*sel[0]),
            pl.ds(*sel[1]),
            pl.ds(pl.multiple_of(sel[2][0] * BLOCK, BLOCK), sel[2][1] * BLOCK),
        )

    def only(base, axis, start, size):
        sel = list(base)
        sel[axis] = (start, size)
        return sel

    own_sel = [(pos[0], 1), (pos[1], 1), (pos[2], 1)]
    full = [(0, 4), (0, 4), (0, 4)]
    ROUTE = ((0,), (3,))
    STRAIGHT = (1, 2)
    STEPS = (0, 1, 3, 2)

    def plane(p, k_last, k_second):
        sel = only(full, ORDER[p][2], along(ORDER[p][2], k_last), 1)
        return only(sel, ORDER[p][1], along(ORDER[p][1], k_second), 1)

    def across_plane(p, q, r):
        at = list(pos)
        at[ORDER[p][0]] = along(ORDER[p][0], q)
        at[ORDER[p][1]] = along(ORDER[p][1], r)
        return device(at, core)

    def gather(buf, blocks, fill_one, fill_two):
        def at(p, sel):
            return buf.at[(g0 + p,) + place(sel)]

        def share(p, sel, to):
            return remote(at(p, sel), at(p, sel), to)

        for p in range(PARTS):
            buf[(g0 + p,) + place(own_sel)] = blocks[p][None, None]
        across = []
        first = [{} for _ in range(PARTS)]
        three = [[{}, {}, {}] for _ in range(PARTS)]
        four = [[{}, {}] for _ in range(PARTS)]

        def arrived(p, r):
            for q in STEPS:
                if q or r:
                    first[p][q, (4 - r) % 4].wait_recv()

        def to_neighbours(p, r):
            for way, k in ((0, 1), (1, 3)):
                three[p][way][r] = share(p, plane(p, 0, r), peer(ORDER[p][2], k))
            if r in STRAIGHT:
                three[p][2][r] = share(p, plane(p, 0, r), peer(ORDER[p][2], 2))

        def onward(p, way, r):
            k = (1, 3)[way]
            three[p][way][r].wait_recv()
            four[p][way][r] = share(p, plane(p, 4 - k, r), peer(ORDER[p][2], k))

        def over(p, k):
            sel = only(full, ORDER[p][2], along(ORDER[p][2], k), 1)
            across.append(share(p, sel, other))

        for r in STEPS:
            for p in range(PARTS):
                for q in STEPS:
                    if q or r:
                        first[p][q, r] = share(p, own_sel, across_plane(p, q, r))
        fill_one()
        for r in (0, 3, 1):
            for p in range(PARTS):
                arrived(p, r)
                to_neighbours(p, r)
        for p in range(PARTS):
            onward(p, 0, 0)
        for p in range(PARTS):
            arrived(p, 2)
            to_neighbours(p, 2)
            over(p, 0)
        fill_two()
        for p in range(PARTS):
            onward(p, 1, 3)
        for p in range(PARTS):
            three[p][0][3].wait_recv()
            three[p][1][0].wait_recv()
            for r in STRAIGHT:
                for way in range(2):
                    three[p][way][r].wait_recv()
            over(p, 1)
            over(p, 3)
        for p in range(PARTS):
            for copy in (four[p][0][0], three[p][2][1], four[p][1][3], three[p][2][2]):
                copy.wait_recv()
            over(p, 2)
        return across

    def nothing():
        pass

    def turn_dec():
        for copy in load_dec:
            copy.wait()

        @pl.loop(0, 2)
        def _(h):
            for q in range(PARTS):
                dec_t[pl.ds(pl.multiple_of(h * HALF + q * GROUP, 128), GROUP), :] = dec[
                    h, :, q * GROUP : (q + 1) * GROUP
                ].T

        norms[...] = jnp.zeros_like(norms)

        @pl.loop(0, 9)
        def _(r):
            rows = dec_t[pl.ds(pl.multiple_of(r * 256, 256), 256), :].astype(jnp.float32)
            norms[...] += jnp.sum(rows * rows, axis=0, keepdims=True)

        norms[...] = jnp.sqrt(norms[...]) * (l1_coeff / loss_norm)

    def wide(buf, t, of_core):
        return jnp.concatenate(
            [buf[of_core * PARTS + p, t].reshape(TILE, GROUP) for p in range(PARTS)], axis=1
        )

    def half_rows(of_core):
        return pl.ds(pl.multiple_of(of_core * HALF, 128), HALF)

    def product(buf, matrix, across, use):
        @pl.loop(0, ROWS // TILE)
        def _(t):
            half_sum[t] = jnp.dot(
                wide(buf, t, core), matrix[half_rows(core), :], preferred_element_type=jnp.float32
            )

        for copy in across:
            copy.wait_recv()
        for t in range(ROWS // TILE):
            use(
                t,
                half_sum[t]
                + jnp.dot(
                    wide(buf, t, 1 - core),
                    matrix[half_rows(1 - core), :],
                    preferred_element_type=jnp.float32,
                ),
            )

    pl.semaphore_wait(ready, len(greet) - 2)
    across = gather(cen, [own_cen[p] for p in range(PARTS)], nothing, turn_dec)
    load_weight.wait()
    keep_weight = local(weight, kept_out.at[pl.ds(D, D), pl.ds(LAT_DEV, LAT_DEV)])
    crossing = []

    def encode(t, pre):
        codes[t] = jnp.maximum(pre + enc_bias_in[...], 0.0).astype(jnp.bfloat16)
        made = jnp.dot(codes[t], dec[1 - core], preferred_element_type=jnp.float32)
        for p in range(PARTS):
            cross_send[p, t] = (
                made[:, p * GROUP : (p + 1) * GROUP].astype(jnp.bfloat16).reshape(4, 64, GROUP)
            )
        crossing.append(remote(cross_send.at[:, t], cross_recv.at[:, t], other))

    product(cen, weight, across, encode)

    @pl.loop(0, ROWS // TILE)
    def _(t):
        made = jnp.dot(codes[t], dec[core], preferred_element_type=jnp.float32)
        for p in range(PARTS):
            part_sum[p, t] = made[:, p * GROUP : (p + 1) * GROUP].reshape(4, 64, GROUP)

    for copy in crossing:
        copy.wait_recv()

    def here(p, sel):
        where = (p,) + place(sel)
        value = part_sum[where] + cross_recv[where].astype(jnp.float32)
        return value.reshape(-1, GROUP)

    def turn_centered(first, last):
        @pl.loop(0, ROWS // TILE)
        def _(t):
            for g in range(first, last):
                cen_t[g * GROUP : (g + 1) * GROUP, pl.ds(pl.multiple_of(t * TILE, TILE), TILE)] = (
                    cen[g, t].reshape(TILE, GROUP).T
                )

    step_a = [{} for _ in range(PARTS)]
    step_b = [[{}, {}] for _ in range(PARTS)]

    def to_far(p, r, k):
        a_send[p, r] = here(p, plane(p, 2, r)).astype(jnp.bfloat16)
        step_a[p][r] = remote(a_send.at[p, r], a_recv.at[p, r], peer(ORDER[p][2], k))

    def to_owner(p, way, r):
        k = (1, 3)[way]
        value = here(p, plane(p, k, r))
        if r in ROUTE[way]:
            step_a[p][r].wait_recv()
            value = value + a_recv[p, r].astype(jnp.float32)
        b_send[p, way, r] = value.astype(jnp.bfloat16)
        step_b[p][way][r] = remote(b_send.at[p, way, r], b_recv.at[p, way, r], peer(ORDER[p][2], k))

    for way, k in ((0, 1), (1, 3)):
        for r in ROUTE[way]:
            for p in range(PARTS):
                to_far(p, r, k)
    for r in (2, 1):
        for p in range(PARTS):
            to_far(p, r, 2)
            for way in range(2):
                to_owner(p, way, r)
    for way in range(2):
        for r in ROUTE[1 - way]:
            for p in range(PARTS):
                to_owner(p, way, r)
    for way in range(2):
        for r in ROUTE[way]:
            for p in range(PARTS):
                to_owner(p, way, r)
    turn_centered(0, 4)
    step_c = [{} for _ in range(PARTS)]
    for r in (2, 1, 3, 0):
        for p in range(PARTS):
            value = here(p, plane(p, 0, r))
            if r in STRAIGHT:
                step_a[p][r].wait_recv()
                value = value + a_recv[p, r].astype(jnp.float32)
            for way in range(2):
                step_b[p][way][r].wait_recv()
                value = value + b_recv[p, way, r].astype(jnp.float32)
            c_send[p, r] = value.astype(jnp.bfloat16).reshape(4, BLOCK, GROUP)
            if r == 0:
                plane_sum[p] = value.reshape(4, BLOCK, GROUP)
            for q in (2, 1, 3, 0):
                if q or r:
                    step_c[p][q, r] = remote(
                        c_send.at[p, r, along(ORDER[p][0], q)], c_recv.at[p, r, q], across_plane(p, q, r)
                    )
    kept = []
    for p in range(PARTS):
        value = plane_sum[p, pos[ORDER[p][0]]]
        for r in (2, 1, 3, 0):
            for q in STEPS:
                if q or r:
                    step_c[p][q, r].wait_recv()
                    value = value + c_recv[p, r, q].astype(jnp.float32)
        kept.append((value - own_cen[p].astype(jnp.float32)).astype(jnp.bfloat16))

    put = [keep_weight]

    def last_turn():
        turn_centered(4, 6)
        put.append(local(cen_t, kept_out.at[pl.ds(0, D)]))

    across = gather(err, kept, nothing, last_turn)

    def slope_of(t, back):
        slope = jnp.where(
            codes[t].astype(jnp.float32) > 0.0, back * (2.0 / loss_norm) + norms[...], 0.0
        )
        slopes[t * TILE : (t + 1) * TILE, :] = slope.astype(jnp.bfloat16)
        put.append(
            local(
                slopes.at[pl.ds(t * TILE, TILE)],
                kept_out.at[pl.ds(D + t * TILE, TILE), pl.ds(0, LAT_DEV)],
            )
        )

    product(err, dec_t, across, slope_of)
    row = (m * 32 + lat) * 8
    holder = lax.div(row, 32)
    hx = lax.div(lax.rem(row, 32), BLOCK) * 2 + lax.rem(holder, 2)
    hyz = lax.div(holder, 2)
    hz = pl.ds(pl.multiple_of(lax.rem(hyz, 4) * BLOCK, BLOCK), BLOCK)
    upper = lax.rem(row, BLOCK) > 0
    for g in range(2 * PARTS):
        rows = err[g, hx, lax.div(hyz, 4), hz, :].astype(jnp.float32)
        rows = jnp.where(upper, rows[8:], rows[:8])
        error_rows[:, g * GROUP : (g + 1) * GROUP] = jnp.concatenate([rows, rows]).astype(jnp.bfloat16)
    for i in range(3):
        put.append(
            local(
                error_rows.at[:, pl.ds(i * 768, 768)],
                kept_out.at[pl.ds(2 * D + i * BLOCK, BLOCK), pl.ds(0, 768)],
            )
        )
    for copy in put:
        copy.wait()
    for copy in sent:
        copy.wait_send()


N_REMOTE = 3 + 2 * PARTS * (15 + 10 + 2 + 4) + 4 + PARTS * (4 + 8 + 15)
N_LOCAL = 4 + 2 + 1 + 1 + 1 + 4 + 3
KEPT = 8192


def exchange(resid, terms, dec_bias, enc_weight, enc_bias, dec_weight):
    bf16, f32 = jnp.bfloat16, jnp.float32
    anywhere = pl.BlockSpec(memory_space=pl.ANY)
    hbm = pl.BlockSpec(memory_space=pltpu.HBM)
    return pl.pallas_call(
        exchange_kernel,
        out_shape=jax.ShapeDtypeStruct((KEPT, ROWS), bf16),
        in_specs=[hbm] * 6,
        out_specs=anywhere,
        scratch_shapes=[
            pltpu.VMEM((6, 4, 4, 64, GROUP), bf16),
            pltpu.VMEM((6, 4, 4, 64, GROUP), bf16),
            pltpu.VMEM((D, ROWS), bf16),
            pltpu.VMEM((D, LAT_DEV), bf16),
            pltpu.VMEM((2, LAT_DEV, HALF), bf16),
            pltpu.VMEM((D, LAT_DEV), bf16),
            pltpu.VMEM((1, LAT_DEV), f32),
            pltpu.VMEM((4, TILE, LAT_DEV), bf16),
            pltpu.VMEM((PARTS, 4, 4, 64, GROUP), bf16),
            pltpu.VMEM((PARTS, 4, 4, 64, GROUP), bf16),
            pltpu.VMEM((PARTS, 4, 4, 64, GROUP), f32),
            pltpu.VMEM((PARTS, 4, 64, GROUP), bf16),
            pltpu.VMEM((PARTS, 4, 64, GROUP), bf16),
            pltpu.VMEM((PARTS, 2, 4, 64, GROUP), bf16),
            pltpu.VMEM((PARTS, 2, 4, 64, GROUP), bf16),
            pltpu.VMEM((PARTS, 4, 4, BLOCK, GROUP), bf16),
            pltpu.VMEM((PARTS, 4, 4, BLOCK, GROUP), bf16),
            pltpu.VMEM((PARTS, 4, BLOCK, GROUP), f32),
            pltpu.VMEM((ROWS, LAT_DEV), bf16),
            pltpu.VMEM((4, TILE, LAT_DEV), f32),
            pltpu.VMEM((4, BLOCK, HALF), bf16),
            pltpu.VMEM((BLOCK, HALF), bf16),
            pltpu.VMEM((D,), f32),
            pltpu.VMEM((1, LAT_DEV), f32),
            pltpu.VMEM((PARTS, BLOCK, GROUP), bf16),
            pltpu.VMEM((BLOCK, D), bf16),
            pltpu.SemaphoreType.DMA((N_REMOTE,)),
            pltpu.SemaphoreType.DMA((N_REMOTE,)),
            pltpu.SemaphoreType.DMA((N_LOCAL,)),
            pltpu.SemaphoreType.REGULAR,
        ],
        cost_estimate=pl.CostEstimate(flops=90_000_000_000, bytes_accessed=10_000_000, transcendentals=0),
        compiler_params=pltpu.CompilerParams(
            collective_id=0, has_side_effects=True, vmem_limit_bytes=54 * 1024 * 1024
        ),
    )(resid, terms, dec_bias, enc_weight, enc_bias, dec_weight)


STEP_ROWS = 384
TILES = D // STEP_ROWS


def adam_kernel(
    kept, first, second,
    weight_new, first_new, second_new, error_new,
    cen_in, slopes_in, weight_in, one_in, two_in, error_in, weight_out, one_out, two_out,
    in_sems, out_sems, lone_sems,
):
    def tile(t):
        return pl.ds(t * STEP_ROWS, STEP_ROWS)

    load_slopes = pltpu.make_async_copy(
        kept.at[pl.ds(D, ROWS), pl.ds(0, LAT_DEV)], slopes_in, lone_sems.at[0]
    )
    load_slopes.start()
    loads = []
    for t in range(TILES):
        pairs = (
            (kept.at[tile(t)], cen_in),
            (kept.at[pl.ds(D + t * STEP_ROWS, STEP_ROWS), pl.ds(LAT_DEV, LAT_DEV)], weight_in),
            (first.at[tile(t)], one_in),
            (second.at[tile(t)], two_in),
        )
        step = [
            pltpu.make_async_copy(src, dst.at[tile(t)], in_sems.at[i, t])
            for i, (src, dst) in enumerate(pairs)
        ]
        for copy in step:
            copy.start()
        loads.append(step)
    load_error = [
        pltpu.make_async_copy(
            kept.at[pl.ds(2 * D + i * BLOCK, BLOCK), pl.ds(0, 768)],
            error_in.at[:, pl.ds(i * 768, 768)],
            lone_sems.at[1 + i],
        )
        for i in range(3)
    ]
    for copy in load_error:
        copy.start()
    load_slopes.wait()
    corr_one = 1.0 - beta_one**STEP
    corr_two = 1.0 - beta_two**STEP
    stores = []
    for t in range(TILES):
        for copy in loads[t]:
            copy.wait()
        rows = tile(t)
        grad = jnp.dot(cen_in[rows], slopes_in[...], preferred_element_type=jnp.float32)
        one = beta_one * one_in[rows] + (1.0 - beta_one) * grad
        two = beta_two * two_in[rows] + (1.0 - beta_two) * grad * grad
        one_out[rows] = one
        two_out[rows] = two
        scaled = two * (1.0 / corr_two)
        change = one * (learn_rate / corr_one) / (scaled * lax.rsqrt(scaled) + adam_eps)
        weight_out[rows] = (weight_in[rows].astype(jnp.float32) - change).astype(jnp.bfloat16)
        pairs = ((one_out, first_new), (two_out, second_new), (weight_out, weight_new))
        for i, (src, dst) in enumerate(pairs):
            copy = pltpu.make_async_copy(src.at[rows], dst.at[rows], out_sems.at[i, t])
            copy.start()
            stores.append(copy)
    for copy in load_error:
        copy.wait()
    error_new[...] = error_in[:8, :]
    for copy in stores:
        copy.wait()


def adam(kept, first, second):
    bf16, f32 = jnp.bfloat16, jnp.float32
    anywhere = pl.BlockSpec(memory_space=pl.ANY)
    hbm = pl.BlockSpec(memory_space=pltpu.HBM)
    return pl.pallas_call(
        adam_kernel,
        out_shape=(
            jax.ShapeDtypeStruct((D, LAT_DEV), bf16),
            jax.ShapeDtypeStruct((D, LAT_DEV), f32),
            jax.ShapeDtypeStruct((D, LAT_DEV), f32),
            jax.ShapeDtypeStruct((8, D), bf16),
        ),
        in_specs=[anywhere] * 3,
        out_specs=(hbm, hbm, hbm, pl.BlockSpec(memory_space=pltpu.VMEM)),
        scratch_shapes=[
            pltpu.VMEM((D, ROWS), bf16),
            pltpu.VMEM((ROWS, LAT_DEV), bf16),
            pltpu.VMEM((D, LAT_DEV), bf16),
            pltpu.VMEM((D, LAT_DEV), f32),
            pltpu.VMEM((D, LAT_DEV), f32),
            pltpu.VMEM((BLOCK, D), bf16),
            pltpu.VMEM((D, LAT_DEV), bf16),
            pltpu.VMEM((D, LAT_DEV), f32),
            pltpu.VMEM((D, LAT_DEV), f32),
            pltpu.SemaphoreType.DMA((4, TILES)),
            pltpu.SemaphoreType.DMA((3, TILES)),
            pltpu.SemaphoreType.DMA((4,)),
        ],
        cost_estimate=pl.CostEstimate(
            flops=2 * ROWS * D * LAT_DEV, bytes_accessed=29_000_000, transcendentals=0
        ),
        compiler_params=pltpu.CompilerParams(vmem_limit_bytes=44 * 1024 * 1024),
    )(kept, first, second)


def on_device(
    resid_in, layer_terms, dec_bias, enc_weight, enc_bias, dec_weight, first_moment, second_moment
):
    kept = exchange(
        resid_in, layer_terms, dec_bias, enc_weight, enc_bias[None], dec_weight
    )
    return adam(kept, first_moment, second_moment)


def solution(mesh):
    in_specs = (
        P("lat", None),
        P("mp", "lat", None),
        P(),
        P(None, ("mp", "lat")),
        P(("mp", "lat")),
        P(("mp", "lat"), None),
        P(None, ("mp", "lat")),
        P(None, ("mp", "lat")),
    )
    out_specs = (
        P(None, ("mp", "lat")),
        P(None, ("mp", "lat")),
        P(None, ("mp", "lat")),
        P(("mp", "lat"), None),
    )
    return jax.shard_map(
        on_device, mesh=mesh, in_specs=in_specs, out_specs=out_specs, check_vma=False
    )
```

```python
import jax
import jax.numpy as jnp
from jax import lax
from jax.experimental import pallas as pl
from jax.experimental.pallas import tpu as pltpu
from jax.sharding import PartitionSpec as P

MESH = pl.DeviceIdType.MESH
STEP = 10
l1_coeff = 5.0
loss_norm = 32.0
beta_one = 0.9
beta_two = 0.95
learn_rate = 0.001
adam_eps = 1e-08

D = 2304
HALF = D // 2
GROUP = HALF // 3
PARTS = 3
PIECES = 2
LAT_DEV = 512
ROWS = 1024
BLOCK = 16
TILE = 256
ORDER = ((2, 1, 0), (0, 2, 1), (1, 0, 2))


def exchange_kernel(
    resid, terms, dec_bias, enc_weight, enc_bias, dec_weight,
    kept_out,
    cen, err, cen_t, weight, dec, dec_t, norms, codes, cross_send, cross_recv, part_sum,
    b_send, b_recv, c_send, c_recv, plane_sum, slopes, half_sum,
    term_in, resid_in, bias_in, enc_bias_in, own_cen, error_rows,
    send_sems, recv_sems, local_sems, ready,
):
    m = lax.axis_index("mp")
    lat = lax.axis_index("lat")
    core = lax.rem(m, 2)
    yz = lax.div(lat, 2)
    x = lax.div(m, 2) * 2 + lax.rem(lat, 2)
    pos = (x, lax.div(yz, 4), lax.rem(yz, 4))

    def device(at, on_core):
        return (lax.div(at[0], 2) * 2 + on_core, (at[1] * 4 + at[2]) * 2 + lax.rem(at[0], 2))

    def along(axis, k):
        return lax.rem(pos[axis] + k, 4)

    def peer(axis, k):
        at = list(pos)
        at[axis] = along(axis, k)
        return device(at, core)

    other = device(pos, 1 - core)
    g0 = core * PARTS

    count = [0, 0]
    sent = []

    def remote(src, dst, to):
        i = count[0]
        count[0] += 1
        copy = pltpu.make_async_remote_copy(
            src_ref=src, dst_ref=dst, send_sem=send_sems.at[i], recv_sem=recv_sems.at[i],
            device_id=to, device_id_type=MESH,
        )
        copy.start()
        sent.append(copy)
        return copy

    def local(src, dst):
        i = count[1]
        count[1] += 1
        copy = pltpu.make_async_copy(src, dst, local_sems.at[i])
        copy.start()
        return copy

    rows16 = pl.ds(pl.multiple_of(lax.div(m, 2) * BLOCK, BLOCK), BLOCK)
    half = pl.ds(pl.multiple_of(core * HALF, 128), HALF)
    early = [
        local(terms.at[0, rows16, half], term_in.at[0]),
        local(resid.at[rows16, half], resid_in),
        local(dec_bias, bias_in),
        local(enc_bias, enc_bias_in),
    ]
    load_dec = [local(dec_weight.at[:, pl.ds(h * HALF, HALF)], dec.at[h]) for h in range(2)]
    load_weight = local(enc_weight, weight)

    barrier = pltpu.get_barrier_semaphore()
    greet = [other, device((lax.rem(x + 2, 4), pos[1], pos[2]), 1 - core)]
    greet += [peer(axis, k) for axis in range(3) for k in (1, 2, 3)]
    for to in greet:
        pl.semaphore_signal(barrier, inc=1, device_id=to, device_id_type=MESH)
    pl.semaphore_wait(barrier, len(greet))
    for to in greet[2:]:
        pl.semaphore_signal(ready, inc=1, device_id=to, device_id_type=MESH)

    moves = []
    for k in (1, 2, 3):
        mt = lax.rem(m + k, 4)
        moves.append(
            remote(
                terms.at[
                    0,
                    pl.ds(pl.multiple_of(lax.div(mt, 2) * BLOCK, BLOCK), BLOCK),
                    pl.ds(pl.multiple_of(lax.rem(mt, 2) * HALF, 128), HALF),
                ],
                term_in.at[k],
                (mt, lat),
            )
        )
    for copy in early:
        copy.wait()
    for copy in moves:
        copy.wait_recv()
    total = term_in[0].astype(jnp.float32)
    for k in (1, 2, 3):
        total = total + term_in[k].astype(jnp.float32)
    bias = bias_in[...].reshape(1, D)
    bias = jnp.where(core == 0, bias[:, :HALF], bias[:, HALF:])
    own = (resid_in[...].astype(jnp.float32) + total - bias).astype(jnp.bfloat16)
    for p in range(PARTS):
        own_cen[p] = own[:, p * GROUP : (p + 1) * GROUP]

    def place(sel):
        return (
            pl.ds(*sel[0]),
            pl.ds(*sel[1]),
            pl.ds(pl.multiple_of(sel[2][0] * BLOCK, BLOCK), sel[2][1] * BLOCK),
        )

    def only(base, axis, start, size):
        sel = list(base)
        sel[axis] = (start, size)
        return sel

    own_sel = [(pos[0], 1), (pos[1], 1), (pos[2], 1)]
    full = [(0, 4), (0, 4), (0, 4)]
    ROUTE = ((0,), (3,))
    STRAIGHT = (1, 2)
    STEPS = (0, 1, 3, 2)

    def plane(p, k_last, k_second):
        sel = only(full, ORDER[p][2], along(ORDER[p][2], k_last), 1)
        return only(sel, ORDER[p][1], along(ORDER[p][1], k_second), 1)

    def across_plane(p, q, r):
        at = list(pos)
        at[ORDER[p][0]] = along(ORDER[p][0], q)
        at[ORDER[p][1]] = along(ORDER[p][1], r)
        return device(at, core)

    def gather(buf, blocks, fill_one, fill_two):
        def at(p, sel):
            return buf.at[(g0 + p,) + place(sel)]

        def share(p, sel, to):
            return remote(at(p, sel), at(p, sel), to)

        for p in range(PARTS):
            buf[(g0 + p,) + place(own_sel)] = blocks[p][None, None]
        across = []
        first = [{} for _ in range(PARTS)]
        three = [[{}, {}, {}] for _ in range(PARTS)]
        four = [[{}, {}] for _ in range(PARTS)]

        def arrived(p, r):
            for q in STEPS:
                if q or r:
                    first[p][q, (4 - r) % 4].wait_recv()

        def to_neighbours(p, r):
            for way, k in ((0, 1), (1, 3)):
                three[p][way][r] = share(p, plane(p, 0, r), peer(ORDER[p][2], k))
            if r in STRAIGHT:
                three[p][2][r] = share(p, plane(p, 0, r), peer(ORDER[p][2], 2))

        def onward(p, way, r):
            k = (1, 3)[way]
            three[p][way][r].wait_recv()
            four[p][way][r] = share(p, plane(p, 4 - k, r), peer(ORDER[p][2], k))

        def over(p, k):
            sel = only(full, ORDER[p][2], along(ORDER[p][2], k), 1)
            across.append(share(p, sel, other))

        for r in STEPS:
            for p in range(PARTS):
                for q in STEPS:
                    if q or r:
                        first[p][q, r] = share(p, own_sel, across_plane(p, q, r))
        fill_one()
        for r in (0, 3, 1):
            for p in range(PARTS):
                arrived(p, r)
                to_neighbours(p, r)
        for p in range(PARTS):
            onward(p, 0, 0)
        for p in range(PARTS):
            arrived(p, 2)
            to_neighbours(p, 2)
            over(p, 0)
        fill_two()
        for p in range(PARTS):
            onward(p, 1, 3)
        for p in range(PARTS):
            three[p][0][3].wait_recv()
            three[p][1][0].wait_recv()
            for r in STRAIGHT:
                for way in range(2):
                    three[p][way][r].wait_recv()
            over(p, 1)
            over(p, 3)
        for p in range(PARTS):
            for copy in (four[p][0][0], three[p][2][1], four[p][1][3], three[p][2][2]):
                copy.wait_recv()
            over(p, 2)
        return across

    def nothing():
        pass

    def turn_dec():
        for copy in load_dec:
            copy.wait()

        @pl.loop(0, 2)
        def _(h):
            for q in range(PARTS):
                dec_t[pl.ds(pl.multiple_of(h * HALF + q * GROUP, 128), GROUP), :] = dec[
                    h, :, q * GROUP : (q + 1) * GROUP
                ].T

        norms[...] = jnp.zeros_like(norms)

        @pl.loop(0, 9)
        def _(r):
            rows = dec_t[pl.ds(pl.multiple_of(r * 256, 256), 256), :].astype(jnp.float32)
            norms[...] += jnp.sum(rows * rows, axis=0, keepdims=True)

        norms[...] = jnp.sqrt(norms[...]) * (l1_coeff / loss_norm)

    def wide(buf, t, of_core):
        return jnp.concatenate(
            [buf[of_core * PARTS + p, t].reshape(TILE, GROUP) for p in range(PARTS)], axis=1
        )

    def half_rows(of_core):
        return pl.ds(pl.multiple_of(of_core * HALF, 128), HALF)

    def product(buf, matrix, across, use):
        @pl.loop(0, ROWS // TILE)
        def _(t):
            half_sum[t] = jnp.dot(
                wide(buf, t, core), matrix[half_rows(core), :], preferred_element_type=jnp.float32
            )

        for copy in across:
            copy.wait_recv()
        for t in range(ROWS // TILE):
            use(
                t,
                half_sum[t]
                + jnp.dot(
                    wide(buf, t, 1 - core),
                    matrix[half_rows(1 - core), :],
                    preferred_element_type=jnp.float32,
                ),
            )

    pl.semaphore_wait(ready, len(greet) - 2)
    across = gather(cen, [own_cen[p] for p in range(PARTS)], nothing, turn_dec)
    load_weight.wait()
    keep_weight = local(weight, kept_out.at[pl.ds(D, D), pl.ds(LAT_DEV, LAT_DEV)])
    crossing = []

    def encode(t, pre):
        codes[t] = jnp.maximum(pre + enc_bias_in[...], 0.0).astype(jnp.bfloat16)
        made = jnp.dot(codes[t], dec[1 - core], preferred_element_type=jnp.float32)
        for p in range(PARTS):
            cross_send[p, t] = (
                made[:, p * GROUP : (p + 1) * GROUP].astype(jnp.bfloat16).reshape(4, 64, GROUP)
            )
        crossing.append(remote(cross_send.at[:, t], cross_recv.at[:, t], other))

    product(cen, weight, across, encode)

    @pl.loop(0, ROWS // TILE)
    def _(t):
        made = jnp.dot(codes[t], dec[core], preferred_element_type=jnp.float32)
        for p in range(PARTS):
            part_sum[p, t] = made[:, p * GROUP : (p + 1) * GROUP].reshape(4, 64, GROUP)

    for copy in crossing:
        copy.wait_recv()

    def here(p, sel):
        where = (p,) + place(sel)
        value = part_sum[where] + cross_recv[where].astype(jnp.float32)
        return value.reshape(-1, GROUP)

    def turn_centered(first, last):
        @pl.loop(0, ROWS // TILE)
        def _(t):
            for g in range(first, last):
                cen_t[g * GROUP : (g + 1) * GROUP, pl.ds(pl.multiple_of(t * TILE, TILE), TILE)] = (
                    cen[g, t].reshape(TILE, GROUP).T
                )

    slots = (2, 1, 3, 0)
    step_a = [[{} for _ in range(PIECES)] for _ in range(PARTS)]
    width = 4 // PIECES
    for piece in range(PIECES):
        inside = pl.ds(piece * width, width)
        for way, k in enumerate((2, 1, 3)):
            for p in range(PARTS):
                for slot in range(piece * width, (piece + 1) * width):
                    b_send[p, way, slot] = here(p, plane(p, k, slots[slot])).astype(jnp.bfloat16)
                step_a[p][piece][way] = remote(
                    b_send.at[p, way, inside], b_recv.at[p, way, inside], peer(ORDER[p][2], k)
                )
    turn_centered(0, 4)
    step_c = [{} for _ in range(PARTS)]
    for slot, r in enumerate(slots):
        for p in range(PARTS):
            value = here(p, plane(p, 0, r))
            for way in range(3):
                if slot % width == 0:
                    step_a[p][slot // width][way].wait_recv()
                value = value + b_recv[p, way, slot].astype(jnp.float32)
            c_send[p, r] = value.astype(jnp.bfloat16).reshape(4, BLOCK, GROUP)
            if r == 0:
                plane_sum[p] = value.reshape(4, BLOCK, GROUP)
            for q in (2, 1, 3, 0):
                if q or r:
                    step_c[p][q, r] = remote(
                        c_send.at[p, r, along(ORDER[p][0], q)], c_recv.at[p, r, q], across_plane(p, q, r)
                    )
    kept = []
    for p in range(PARTS):
        value = plane_sum[p, pos[ORDER[p][0]]]
        for r in (2, 1, 3, 0):
            for q in STEPS:
                if q or r:
                    step_c[p][q, r].wait_recv()
                    value = value + c_recv[p, r, q].astype(jnp.float32)
        kept.append((value - own_cen[p].astype(jnp.float32)).astype(jnp.bfloat16))

    put = [keep_weight]

    def last_turn():
        turn_centered(4, 6)
        put.append(local(cen_t, kept_out.at[pl.ds(0, D)]))

    across = gather(err, kept, nothing, last_turn)

    def slope_of(t, back):
        slope = jnp.where(
            codes[t].astype(jnp.float32) > 0.0, back * (2.0 / loss_norm) + norms[...], 0.0
        )
        slopes[t * TILE : (t + 1) * TILE, :] = slope.astype(jnp.bfloat16)
        put.append(
            local(
                slopes.at[pl.ds(t * TILE, TILE)],
                kept_out.at[pl.ds(D + t * TILE, TILE), pl.ds(0, LAT_DEV)],
            )
        )

    product(err, dec_t, across, slope_of)
    row = (m * 32 + lat) * 8
    holder = lax.div(row, 32)
    hx = lax.div(lax.rem(row, 32), BLOCK) * 2 + lax.rem(holder, 2)
    hyz = lax.div(holder, 2)
    hz = pl.ds(pl.multiple_of(lax.rem(hyz, 4) * BLOCK, BLOCK), BLOCK)
    upper = lax.rem(row, BLOCK) > 0
    for g in range(2 * PARTS):
        rows = err[g, hx, lax.div(hyz, 4), hz, :].astype(jnp.float32)
        rows = jnp.where(upper, rows[8:], rows[:8])
        error_rows[:, g * GROUP : (g + 1) * GROUP] = jnp.concatenate([rows, rows]).astype(jnp.bfloat16)
    for i in range(3):
        put.append(
            local(
                error_rows.at[:, pl.ds(i * 768, 768)],
                kept_out.at[pl.ds(2 * D + i * BLOCK, BLOCK), pl.ds(0, 768)],
            )
        )
    for copy in put:
        copy.wait()
    for copy in sent:
        copy.wait_send()


N_REMOTE = 3 + 2 * PARTS * (15 + 10 + 2 + 4) + 4 + PARTS * (3 * PIECES + 15)
N_LOCAL = 4 + 2 + 1 + 1 + 1 + 4 + 3
KEPT = 8192


def exchange(resid, terms, dec_bias, enc_weight, enc_bias, dec_weight):
    bf16, f32 = jnp.bfloat16, jnp.float32
    anywhere = pl.BlockSpec(memory_space=pl.ANY)
    hbm = pl.BlockSpec(memory_space=pltpu.HBM)
    return pl.pallas_call(
        exchange_kernel,
        out_shape=jax.ShapeDtypeStruct((KEPT, ROWS), bf16),
        in_specs=[hbm] * 6,
        out_specs=anywhere,
        scratch_shapes=[
            pltpu.VMEM((6, 4, 4, 64, GROUP), bf16),
            pltpu.VMEM((6, 4, 4, 64, GROUP), bf16),
            pltpu.VMEM((D, ROWS), bf16),
            pltpu.VMEM((D, LAT_DEV), bf16),
            pltpu.VMEM((2, LAT_DEV, HALF), bf16),
            pltpu.VMEM((D, LAT_DEV), bf16),
            pltpu.VMEM((1, LAT_DEV), f32),
            pltpu.VMEM((4, TILE, LAT_DEV), bf16),
            pltpu.VMEM((PARTS, 4, 4, 64, GROUP), bf16),
            pltpu.VMEM((PARTS, 4, 4, 64, GROUP), bf16),
            pltpu.VMEM((PARTS, 4, 4, 64, GROUP), f32),
            pltpu.VMEM((PARTS, 3, 4, 64, GROUP), bf16),
            pltpu.VMEM((PARTS, 3, 4, 64, GROUP), bf16),
            pltpu.VMEM((PARTS, 4, 4, BLOCK, GROUP), bf16),
            pltpu.VMEM((PARTS, 4, 4, BLOCK, GROUP), bf16),
            pltpu.VMEM((PARTS, 4, BLOCK, GROUP), f32),
            pltpu.VMEM((ROWS, LAT_DEV), bf16),
            pltpu.VMEM((4, TILE, LAT_DEV), f32),
            pltpu.VMEM((4, BLOCK, HALF), bf16),
            pltpu.VMEM((BLOCK, HALF), bf16),
            pltpu.VMEM((D,), f32),
            pltpu.VMEM((1, LAT_DEV), f32),
            pltpu.VMEM((PARTS, BLOCK, GROUP), bf16),
            pltpu.VMEM((BLOCK, D), bf16),
            pltpu.SemaphoreType.DMA((N_REMOTE,)),
            pltpu.SemaphoreType.DMA((N_REMOTE,)),
            pltpu.SemaphoreType.DMA((N_LOCAL,)),
            pltpu.SemaphoreType.REGULAR,
        ],
        cost_estimate=pl.CostEstimate(flops=90_000_000_000, bytes_accessed=10_000_000, transcendentals=0),
        compiler_params=pltpu.CompilerParams(
            collective_id=0, has_side_effects=True, vmem_limit_bytes=54 * 1024 * 1024
        ),
    )(resid, terms, dec_bias, enc_weight, enc_bias, dec_weight)


STEP_ROWS = 384
TILES = D // STEP_ROWS


def adam_kernel(
    kept, first, second,
    weight_new, first_new, second_new, error_new,
    cen_in, slopes_in, weight_in, one_in, two_in, error_in, weight_out, one_out, two_out,
    in_sems, out_sems, lone_sems,
):
    def tile(t):
        return pl.ds(t * STEP_ROWS, STEP_ROWS)

    load_slopes = pltpu.make_async_copy(
        kept.at[pl.ds(D, ROWS), pl.ds(0, LAT_DEV)], slopes_in, lone_sems.at[0]
    )
    load_slopes.start()
    loads = []
    for t in range(TILES):
        pairs = (
            (kept.at[tile(t)], cen_in),
            (kept.at[pl.ds(D + t * STEP_ROWS, STEP_ROWS), pl.ds(LAT_DEV, LAT_DEV)], weight_in),
            (first.at[tile(t)], one_in),
            (second.at[tile(t)], two_in),
        )
        step = [
            pltpu.make_async_copy(src, dst.at[tile(t)], in_sems.at[i, t])
            for i, (src, dst) in enumerate(pairs)
        ]
        for copy in step:
            copy.start()
        loads.append(step)
    load_error = [
        pltpu.make_async_copy(
            kept.at[pl.ds(2 * D + i * BLOCK, BLOCK), pl.ds(0, 768)],
            error_in.at[:, pl.ds(i * 768, 768)],
            lone_sems.at[1 + i],
        )
        for i in range(3)
    ]
    for copy in load_error:
        copy.start()
    load_slopes.wait()
    corr_one = 1.0 - beta_one**STEP
    corr_two = 1.0 - beta_two**STEP
    stores = []
    for t in range(TILES):
        for copy in loads[t]:
            copy.wait()
        rows = tile(t)
        grad = jnp.dot(cen_in[rows], slopes_in[...], preferred_element_type=jnp.float32)
        one = beta_one * one_in[rows] + (1.0 - beta_one) * grad
        two = beta_two * two_in[rows] + (1.0 - beta_two) * grad * grad
        one_out[rows] = one
        two_out[rows] = two
        scaled = two * (1.0 / corr_two)
        change = one * (learn_rate / corr_one) / (scaled * lax.rsqrt(scaled) + adam_eps)
        weight_out[rows] = (weight_in[rows].astype(jnp.float32) - change).astype(jnp.bfloat16)
        pairs = ((one_out, first_new), (two_out, second_new), (weight_out, weight_new))
        for i, (src, dst) in enumerate(pairs):
            copy = pltpu.make_async_copy(src.at[rows], dst.at[rows], out_sems.at[i, t])
            copy.start()
            stores.append(copy)
    for copy in load_error:
        copy.wait()
    error_new[...] = error_in[:8, :]
    for copy in stores:
        copy.wait()


def adam(kept, first, second):
    bf16, f32 = jnp.bfloat16, jnp.float32
    anywhere = pl.BlockSpec(memory_space=pl.ANY)
    hbm = pl.BlockSpec(memory_space=pltpu.HBM)
    return pl.pallas_call(
        adam_kernel,
        out_shape=(
            jax.ShapeDtypeStruct((D, LAT_DEV), bf16),
            jax.ShapeDtypeStruct((D, LAT_DEV), f32),
            jax.ShapeDtypeStruct((D, LAT_DEV), f32),
            jax.ShapeDtypeStruct((8, D), bf16),
        ),
        in_specs=[anywhere] * 3,
        out_specs=(hbm, hbm, hbm, pl.BlockSpec(memory_space=pltpu.VMEM)),
        scratch_shapes=[
            pltpu.VMEM((D, ROWS), bf16),
            pltpu.VMEM((ROWS, LAT_DEV), bf16),
            pltpu.VMEM((D, LAT_DEV), bf16),
            pltpu.VMEM((D, LAT_DEV), f32),
            pltpu.VMEM((D, LAT_DEV), f32),
            pltpu.VMEM((BLOCK, D), bf16),
            pltpu.VMEM((D, LAT_DEV), bf16),
            pltpu.VMEM((D, LAT_DEV), f32),
            pltpu.VMEM((D, LAT_DEV), f32),
            pltpu.SemaphoreType.DMA((4, TILES)),
            pltpu.SemaphoreType.DMA((3, TILES)),
            pltpu.SemaphoreType.DMA((4,)),
        ],
        cost_estimate=pl.CostEstimate(
            flops=2 * ROWS * D * LAT_DEV, bytes_accessed=29_000_000, transcendentals=0
        ),
        compiler_params=pltpu.CompilerParams(vmem_limit_bytes=44 * 1024 * 1024),
    )(kept, first, second)


def on_device(
    resid_in, layer_terms, dec_bias, enc_weight, enc_bias, dec_weight, first_moment, second_moment
):
    kept = exchange(
        resid_in, layer_terms, dec_bias, enc_weight, enc_bias[None], dec_weight
    )
    return adam(kept, first_moment, second_moment)


def solution(mesh):
    in_specs = (
        P("lat", None),
        P("mp", "lat", None),
        P(),
        P(None, ("mp", "lat")),
        P(("mp", "lat")),
        P(("mp", "lat"), None),
        P(None, ("mp", "lat")),
        P(None, ("mp", "lat")),
    )
    out_specs = (
        P(None, ("mp", "lat")),
        P(None, ("mp", "lat")),
        P(None, ("mp", "lat")),
        P(("mp", "lat"), None),
    )
    return jax.shard_map(
        on_device, mesh=mesh, in_specs=in_specs, out_specs=out_specs, check_vma=False
    )
```
